32 devices in a mesh: shots: 4 (over y, x), space: 8 (over z, core).
Axes of the slice: x: 2, y: 2, z: 4, core: 2. Of those that a mesh axis runs over, the one named last changes fastest.
Arguments:
- probes: bfloat16 [8, 64, 2, 128, 8, 128], P('shots', None, None, 'space'), may hold values from -6 to 6
- sources: bfloat16 [8, 2, 128, 8, 128], P('shots', None, 'space'), may hold values from -6 to 6
- sketch: bfloat16 [32, 64, 64], P('space'), may hold values from -6 to 6
- pairing: int32 [8], replicated, may hold values from 0 to 7, each once
Outputs:
- basis: bfloat16 [32, 64, 64], P('space', 'shots')
The draws below stay inside these ranges and needn't reach their ends.
Inputs may be any that keep to these rules, and one draw needn't show every extreme that they name: `pairing`: a permutation of the 8 shot groups.
All inputs are finite; a program needn't handle non-finite values.
Results may differ from the reference program's by a relative error of at most 0.013.
Values may be sent and summed in bfloat16 or wider, within the bound.
No kernel may reach another device: no remote copies, remote signals or barrier semaphores. Data moves between devices by JAX's collectives and lax.ppermute only.
A program may use at most 64 MiB of HBM per device.

```python
import math
import jax
import jax.numpy as jnp
from jax import lax

R = 64
NT = 2
CY = 2
CZ = 32
GROUPS = 8
NXC = 32
NXF = 128
FY = 8
FZ = 128


def block_levels(key, dims, shards, least, high):
    def one(axis_at, blocks):
        steps = jax.random.uniform(jax.random.fold_in(jax.random.fold_in(key, 6), axis_at), (blocks,), jnp.float32, least / len(shards), high / len(shards))
        return jnp.repeat(jnp.exp(steps), dims[axis_at] // blocks).reshape((-1,) + (1,) * (len(dims) - axis_at - 1))

    gain = one(*shards[0])
    for cut in shards[1:]:
        gain = gain * one(*cut)
    return gain


def gaussian(stream_key, dims, scale, reach, cuts=(), held_as=jnp.bfloat16):
    loudness = block_levels(stream_key, dims, cuts, -0.22, 0.18) if cuts else 1.0
    entries = jax.random.normal(stream_key, dims, jnp.float32) * scale * loudness
    return jnp.minimum(jnp.maximum(entries, -reach), reach).astype(held_as)


def setup_inputs(seed: int = 0) -> dict:
    key_of = jax.random.split(jax.random.key(seed), 5)
    return {
        "probes": gaussian(key_of[0], (GROUPS, R, NT, NXF, FY, FZ), 1.0, 6.0, ((0, 4), (3, 8))),
        "sources": gaussian(key_of[1], (GROUPS, NT, NXF, FY, FZ), 1.0, 6.0, ((0, 4), (2, 8))),
        "sketch": gaussian(key_of[2], (NXC, R, CY * CZ), 1.0, 6.0, ((0, 8),)),
        "pairing": jax.random.permutation(key_of[3], GROUPS).astype(jnp.int32),
    }


def spline_table(fine_count, coarse_count, fine_start, coarse_start):
    fine_pos = jnp.arange(fine_count, dtype=jnp.float32) + fine_start
    coarse_pos = jnp.arange(coarse_count, dtype=jnp.float32) + coarse_start
    distance = jnp.abs((fine_pos[:, None] + 0.5 - 4.0 * coarse_pos[None, :] - 2.0) / 4.0)
    inner_part = 2.0 / 3.0 - distance ** 2 + 0.5 * distance ** 3
    outer_part = jnp.maximum(2.0 - distance, 0.0) ** 3 / 6.0
    return jnp.where(distance < 1.0, inner_part, outer_part) / 4.0

def solve_coef(gram_mats, cross_mats):
    rank_size = gram_mats.shape[-1]
    trace_sum = jnp.trace(gram_mats, axis1=1, axis2=2)
    ridge_term = 0.01 * trace_sum / rank_size + 1e-06
    identity = jnp.eye(rank_size, dtype=jnp.float32)
    factor = jnp.linalg.cholesky(gram_mats + ridge_term[:, None, None] * identity)
    halfway = lax.linalg.triangular_solve(factor, cross_mats, left_side=True, lower=True)
    return lax.linalg.triangular_solve(factor, halfway, left_side=True, lower=True, transpose_a=True)

def merge_level(pieces, sketch, scaling):
    hi = lax.Precision.HIGHEST
    piece_wide = pieces.astype(jnp.float32)
    sketch_wide = sketch.astype(jnp.float32)
    gram_mats = jnp.einsum('pxay,pxby->pab', piece_wide, piece_wide, precision=hi)
    cross_mats = jnp.einsum('pxay,xby->pab', piece_wide, sketch_wide, precision=hi)
    coefficients = solve_coef(gram_mats, cross_mats).astype(jnp.bfloat16)
    term_sums = jnp.einsum('pxay,pab->pxby', piece_wide, coefficients.astype(jnp.float32), precision=hi)
    pair_count = pieces.shape[0] // 2
    term_sums = term_sums.reshape((pair_count, 2) + term_sums.shape[1:])
    return (scaling * (term_sums[:, 0] + term_sums[:, 1])).astype(jnp.bfloat16)

def reference(probes, sources, sketch, pairing):
    hi = lax.Precision.HIGHEST
    table_x = spline_table(NXF, NXC, 0, 0)
    table_y = spline_table(FY, CY, 0, 0)
    table_z = spline_table(FZ, CZ, 0, 0)

    def restrict_group(group_data):
        probe_wide = group_data[0].astype(jnp.float32)
        source_wide = group_data[1].astype(jnp.float32)
        images = jnp.einsum('atxyz,txyz->axyz', probe_wide, source_wide, precision=hi)
        images = jnp.einsum('axyz,zc->axyc', images, table_z, precision=hi)
        images = jnp.einsum('axyc,yd->axdc', images, table_y, precision=hi)
        images = jnp.einsum('axdc,xe->aedc', images, table_x, precision=hi)
        images = jnp.transpose(images, (1, 0, 2, 3)).reshape(NXC, R, CY * CZ)
        return images.astype(jnp.bfloat16)
    leaves = lax.map(restrict_group, (probes, sources))
    pieces = jnp.take(leaves, pairing, axis=0)
    scaling = math.sqrt(NXC * CY * CZ / R)
    while pieces.shape[0] > 1:
        pieces = merge_level(pieces, sketch, scaling)
    return pieces[0]
```

```python
import math

import jax
import jax.numpy as jnp
import numpy as np
from jax import lax
from jax.experimental import pallas as pl
from jax.experimental.pallas import tpu as pltpu
from jax.sharding import PartitionSpec as P

F32 = jnp.float32
BF16 = jnp.bfloat16
VMEM_BYTES = 48 << 20


def spline_weights(fine_count, coarse_count, coarse_start):
    fine = np.arange(fine_count, dtype=np.float64)
    coarse = np.arange(coarse_count, dtype=np.float64) + coarse_start
    s = np.abs((fine[:, None] + 0.5 - 4.0 * coarse[None, :] - 2.0) / 4.0)
    inner = 2.0 / 3.0 - s**2 + 0.5 * s**3
    outer = np.maximum(2.0 - s, 0.0) ** 3 / 6.0
    return np.where(s < 1.0, inner, outer) / 4.0


def two_terms(table):
    table = jnp.asarray(table, F32)
    high = table.astype(BF16)
    return high, (table - high.astype(F32)).astype(BF16)


def halves(x):
    high = x.astype(BF16)
    return high, (x - high.astype(F32)).astype(BF16)


def thirds(x):
    high = x.astype(BF16)
    rest = x - high.astype(F32)
    mid = rest.astype(BF16)
    return high, mid, (rest - mid.astype(F32)).astype(BF16)


def dot(a, b):
    return jnp.dot(a, b, preferred_element_type=F32)


def dot_nt(a, b):
    return lax.dot_general(a, b, (((1,), (1,)), ((), ())), preferred_element_type=F32)


def wide_dot(wide, exact):
    return sum(dot(part, exact) for part in thirds(wide))


def dot_wide(exact, wide):
    return sum(dot(exact, part) for part in thirds(wide))


def restrict_kernel(ranks, probes, sources, table_xy, table_z, below, own, above, rows):
    groups, _, fine_z = rows.shape[1] // ranks, None, rows.shape[2]
    cells = sources.shape[1] // 2
    block_ranks = probes.shape[1] // (2 * cells)
    step = pl.program_id(0)
    edges = rows.shape[0]
    for g in range(groups):
        base = g * ranks + step * block_ranks

        def some_ranks(i, _, g=g, base=base):
            parts = []
            for k in range(2):
                at = (2 * i + k) * 2 * cells
                first = probes[g, pl.ds(pl.multiple_of(at, cells), cells)].astype(F32)
                second = probes[g, pl.ds(pl.multiple_of(at + cells, cells), cells)].astype(F32)
                image = first * sources[g, :cells].astype(F32)
                image = image + second * sources[g, cells:].astype(F32)
                parts.append(jnp.concatenate(halves(image), axis=0))
            both = dot(table_xy[...], jnp.concatenate(parts, axis=1))
            both = both[:edges] + both[edges:]
            for k in range(2):
                rows[:, base + 2 * i + k, :] = both[:, k * fine_z : (k + 1) * fine_z]
            return 0

        lax.fori_loop(0, block_ranks // 2, some_ranks, 0, unroll=2)

    @pl.when(step == pl.num_programs(0) - 1)
    def _():
        per = table_z.shape[0] // fine_z
        lanes = table_z.shape[1] // 2
        chunks = []
        for j in range(edges // per):
            total = 0.0
            for r in range(per):
                weights = table_z[r * fine_z : (r + 1) * fine_z]
                for part in halves(rows[j * per + r]):
                    total = total + dot(part, weights)
            chunks.append(total[:, :lanes] + total[:, lanes:])
        below[...] = chunks[0]
        own[...] = jnp.concatenate(chunks[1:-1], axis=1)
        above[...] = chunks[-1]


def restrict(probes, sources):
    groups, ranks, steps_t, fine_x, fine_y, fine_z = probes.shape
    cells = fine_x * fine_y
    coarse_x, coarse_y, coarse_z = fine_x // 4, fine_y // 4, fine_z // 4
    edges_x = coarse_x + 4
    weights_x = spline_weights(fine_x, edges_x, -2)
    weights_y = spline_weights(fine_y, coarse_y, 0)
    weights_z = spline_weights(fine_z, coarse_z, 0)
    table_xy = np.einsum("xe,yd->edxy", weights_x, weights_y).reshape(edges_x * coarse_y, cells)
    high, low = two_terms(table_xy)
    table_xy = jnp.concatenate(
        [jnp.concatenate([high, high], axis=1), jnp.concatenate([low, low], axis=1)], axis=0
    )
    per = 128 // coarse_z
    table_z = np.einsum("zc,rs->rzsc", weights_z, np.eye(per)).reshape(per * fine_z, 128)
    table_z = jnp.concatenate(two_terms(table_z), axis=1)
    block_ranks = 8
    grid = ranks // block_ranks
    block_rows = block_ranks * steps_t * cells
    all_rows = groups * ranks
    lanes = edges_x * coarse_y * coarse_z
    whole = lambda *shape: pl.BlockSpec(shape, lambda i: (0,) * len(shape))
    return pl.pallas_call(
        lambda *refs: restrict_kernel(ranks, *refs),
        grid=(grid,),
        in_specs=[
            pl.BlockSpec((groups, block_rows, fine_z), lambda i: (0, i, 0)),
            whole(groups, steps_t * cells, fine_z),
            whole(*table_xy.shape),
            whole(*table_z.shape),
        ],
        out_specs=[whole(all_rows, 128), whole(all_rows, lanes - 256), whole(all_rows, 128)],
        out_shape=[
            jax.ShapeDtypeStruct((all_rows, 128), F32),
            jax.ShapeDtypeStruct((all_rows, lanes - 256), F32),
            jax.ShapeDtypeStruct((all_rows, 128), F32),
        ],
        scratch_shapes=[pltpu.VMEM((edges_x * coarse_y, all_rows, fine_z), F32)],
        compiler_params=pltpu.CompilerParams(vmem_limit_bytes=VMEM_BYTES),
        name="restrict",
    )(
        probes.reshape(groups, ranks * steps_t * cells, fine_z),
        sources.reshape(groups, steps_t * cells, fine_z),
        table_xy,
        table_z,
    )


def products_kernel(ranks, place, *refs):
    *leaves, sketch, chosen, keep, send, table = refs
    rows = leaves[0].shape[0]
    for i, leaf in enumerate(leaves):
        table[i * rows : (i + 1) * rows, :] = leaf[...]
    picked = chosen.shape[0] // ranks
    for i in range(picked):
        at = pl.multiple_of(place[i] * ranks, ranks)
        chosen[i * ranks : (i + 1) * ranks, :] = table[pl.ds(at, ranks), :]
    pieces = chosen[...]
    gram = dot_nt(pieces, pieces)
    cross = dot_nt(pieces, sketch[...])
    block = lambda i, j: gram[i * ranks : (i + 1) * ranks, j * ranks : (j + 1) * ranks]
    pairs = [(block(i, i), cross[i * ranks : (i + 1) * ranks]) for i in range(picked)]
    pairs += [(block(0, 1), block(2, 3)), (block(0, 2), block(0, 3)), (block(1, 2), block(1, 3))]
    side = place[picked]
    half = ranks // 2
    for n, pair in enumerate(pairs):
        both = jnp.concatenate(pair, axis=1)
        top, bottom = both[:half], both[half:]
        keep[n * half : (n + 1) * half, :] = jnp.where(side == 0, top, bottom)
        send[n * half : (n + 1) * half, :] = jnp.where(side == 0, bottom, top)


def products(leaves, sketch, place, ranks):
    rows, lanes = leaves[0].shape
    count = len(leaves)
    half = (count * rows // ranks // 2) * ranks
    vmem = pl.BlockSpec(memory_space=pltpu.VMEM)
    out_rows = 7 * ranks // 2
    return pl.pallas_call(
        lambda *refs: products_kernel(ranks, *refs),
        in_specs=[pl.BlockSpec(memory_space=pltpu.SMEM)] + [vmem] * (count + 1),
        out_specs=[vmem] * 3,
        out_shape=[
            jax.ShapeDtypeStruct((half, lanes), BF16),
            jax.ShapeDtypeStruct((out_rows, 2 * ranks), F32),
            jax.ShapeDtypeStruct((out_rows, 2 * ranks), F32),
        ],
        scratch_shapes=[pltpu.VMEM((count * rows, lanes), BF16)],
        compiler_params=pltpu.CompilerParams(vmem_limit_bytes=VMEM_BYTES),
        name="products",
    )(place, *leaves, sketch)


def ridge_solve(grams, crosses):
    size = grams[0].shape[0]
    count = len(grams)
    eye = lax.broadcasted_iota(jnp.int32, (size, size), 0) == lax.broadcasted_iota(
        jnp.int32, (size, size), 1
    )
    blocks = size // 8
    whole = []
    for gram, cross in zip(grams, crosses):
        trace = jnp.sum(jnp.where(eye, gram, 0.0))
        gram = gram + jnp.where(eye, 0.01 * trace / size + 1e-06, 0.0)
        whole.append(jnp.concatenate([gram, cross], axis=1))
    start = tuple(
        tuple(m[8 * i : 8 * i + 8] for i in range(blocks)) for m in whole
    )
    sub = lax.broadcasted_iota(jnp.int32, (8, 2 * size), 0)

    def eliminate(_, mats):
        done = []
        for mat in mats:
            head = mat[0]
            columns = [jnp.broadcast_to(head[:, j : j + 1], head.shape) for j in range(8)]
            for j in range(8):
                inverse = 1.0 / columns[j][j : j + 1]
                here = sub == j
                row = head[j : j + 1] * inverse
                head = jnp.where(here, row, head - columns[j] * row)
                for m in range(j + 1, 8):
                    entry = columns[m][j : j + 1] * inverse
                    columns[m] = jnp.where(here, entry, columns[m] - columns[j] * entry)
            rest = []
            for block in mat[1:]:
                new = block
                for j in range(8):
                    new = new - block[:, j : j + 1] * head[j : j + 1]
                rest.append(new)
            done.append(tuple(pltpu.roll(x, 2 * size - 8, 1) for x in rest + [head]))
        return tuple(done)

    mats = lax.fori_loop(0, blocks, eliminate, start)
    return [jnp.concatenate(mat, axis=0)[:, :size].astype(BF16) for mat in mats]


def two_blocks(first, second):
    zero = jnp.zeros_like(first)
    return jnp.concatenate(
        [jnp.concatenate([first, zero], axis=1), jnp.concatenate([zero, second], axis=1)], axis=0
    )


def tree_kernel(ranks, scaling, place, mine, other, pieces, own, send, table):
    half = ranks // 2
    side = place[0]
    for n in range(7):
        a, b = mine[n * half : (n + 1) * half, :], other[n * half : (n + 1) * half, :]
        table[n * ranks : n * ranks + half, :] = jnp.where(side == 0, a, b)
        table[n * ranks + half : (n + 1) * ranks, :] = jnp.where(side == 0, b, a)
    unit = lambda n: table[n * ranks : (n + 1) * ranks, :]
    left = lambda n: unit(n)[:, :ranks]
    right = lambda n: unit(n)[:, ranks:]
    grams = [left(n) for n in range(4)]
    crosses = [right(n) for n in range(4)]
    g01, g23 = left(4), right(4)
    row = lambda *xs: jnp.concatenate(xs, axis=1)
    column = lambda *xs: jnp.concatenate(xs, axis=0)
    corner = column(unit(5), unit(6))
    top = column(row(grams[0], g01), row(g01.T, grams[1]))
    low = column(row(grams[2], g23), row(g23.T, grams[3]))
    joint = column(row(top, corner), row(corner.T, low))
    c = ridge_solve(grams, crosses)
    first = two_blocks(column(c[0], c[1]), column(c[2], c[3]))
    first_t = first.astype(F32).T.astype(BF16)
    square = scaling * scaling
    gram_m = square * dot_wide(first_t, wide_dot(joint, first))
    cross_m = scaling * dot_wide(first_t, column(*crosses))
    d = ridge_solve(
        [gram_m[:ranks, :ranks], gram_m[ranks:, ranks:]], [cross_m[:ranks], cross_m[ranks:]]
    )
    second = column(*d)
    second_t = second.astype(F32).T.astype(BF16)
    gram_n = square * dot_wide(second_t, wide_dot(gram_m, second))
    cross_n = scaling * dot_wide(second_t, cross_m)
    (e,) = ridge_solve([gram_n], [cross_n])
    e_t = e.astype(F32).T.astype(BF16)
    total_t = wide_dot(dot(e_t, second_t), first_t)
    result = (scaling * scaling * scaling) * sum(dot(part, pieces[...]) for part in halves(total_t))
    table[: result.shape[0], :] = result[:, : 2 * ranks]
    table[result.shape[0] : 2 * result.shape[0], :] = result[:, 2 * ranks :]
    count = own.shape[0]
    for out, at in ((own, place[1]), (send, place[2])):
        at = pl.multiple_of(at * count, count)
        for i in range(2):
            out[:, i * 2 * ranks : (i + 1) * 2 * ranks] = table[
                pl.ds(at + i * ranks, count), :
            ]


def tree(mine, other, pieces, place, ranks, scaling, columns):
    vmem = pl.BlockSpec(memory_space=pltpu.VMEM)
    out = jax.ShapeDtypeStruct((columns, pieces.shape[1]), F32)
    return pl.pallas_call(
        lambda *refs: tree_kernel(ranks, scaling, *refs),
        in_specs=[pl.BlockSpec(memory_space=pltpu.SMEM)] + [vmem] * 3,
        out_specs=[vmem] * 2,
        out_shape=[out, out],
        scratch_shapes=[pltpu.VMEM((7 * ranks, 2 * ranks), F32)],
        compiler_params=pltpu.CompilerParams(vmem_limit_bytes=VMEM_BYTES),
        name="tree",
    )(place, mine, other, pieces)


def swap(x, axis, mask):
    return lax.ppermute(x, axis, [(i, i ^ mask) for i in range(lax.axis_size(axis))])


def shift(x, axis, by):
    count = lax.axis_size(axis)
    return lax.ppermute(x, axis, [(i, i + by) for i in range(count) if 0 <= i + by < count])


def body(probes, sources, sketch, pairing):
    groups, ranks = probes.shape[:2]
    coarse_x = probes.shape[3] // 4
    layer = sketch.shape[2]
    shots, space = lax.axis_size("shots"), lax.axis_size("space")
    shot, place = lax.axis_index("shots"), lax.axis_index("space")
    scaling = math.sqrt(coarse_x * space * layer / ranks)

    below, own, above = restrict(probes, sources)
    from_above = shift(below, "space", -1)
    from_below = shift(above, "space", 1)
    leaf = (own + jnp.concatenate([from_below, from_above], axis=1)).astype(BF16)

    leaves = [leaf] + [swap(leaf, "shots", m) for m in range(1, shots)]
    picked = shots * groups // 2
    side = place % 2
    chosen = lax.dynamic_slice_in_dim(pairing, shot // (shots // 2) * picked, picked)
    slots = (chosen // groups ^ shot) * groups + chosen % groups
    sketch_t = jnp.transpose(sketch, (1, 0, 2)).reshape(ranks, coarse_x * layer)
    slots = jnp.concatenate([slots, side[None]]).astype(jnp.int32)
    pieces, mine, send = products(leaves, sketch_t, slots, ranks)

    mine = mine + swap(send, "space", 1)
    mask = 2
    while mask < space:
        mine = mine + swap(mine, "space", mask)
        mask *= 2
    other = swap(mine, "space", 1)

    columns = ranks // shots
    far = shots // 2
    spots = jnp.stack([side, shot, shot ^ far]).astype(jnp.int32)
    own_part, sent = tree(mine, other, pieces, spots, ranks, scaling, columns)
    total = (own_part + swap(sent, "shots", far)).astype(BF16)
    return jnp.transpose(total.reshape(columns, coarse_x, layer), (1, 0, 2))


def solution(mesh):
    in_specs = (
        P("shots", None, None, "space", None, None),
        P("shots", None, "space", None, None),
        P("space", None, None),
        P(),
    )
    out_specs = P("space", "shots", None)
    return jax.shard_map(body, mesh=mesh, in_specs=in_specs, out_specs=out_specs, check_vma=False)
```

```python
import math

import jax
import jax.numpy as jnp
import numpy as np
from jax import lax
from jax.experimental import pallas as pl
from jax.experimental.pallas import tpu as pltpu
from jax.sharding import PartitionSpec as P

F32 = jnp.float32
BF16 = jnp.bfloat16
VMEM_BYTES = 48 << 20
FULL_VMEM = 60 << 20


def spline_weights(fine_count, coarse_count, coarse_start):
    fine = np.arange(fine_count, dtype=np.float64)
    coarse = np.arange(coarse_count, dtype=np.float64) + coarse_start
    s = np.abs((fine[:, None] + 0.5 - 4.0 * coarse[None, :] - 2.0) / 4.0)
    inner = 2.0 / 3.0 - s**2 + 0.5 * s**3
    outer = np.maximum(2.0 - s, 0.0) ** 3 / 6.0
    return np.where(s < 1.0, inner, outer) / 4.0


def two_terms(table):
    table = jnp.asarray(table, F32)
    high = table.astype(BF16)
    return high, (table - high.astype(F32)).astype(BF16)


def halves(x):
    high = x.astype(BF16)
    return high, (x - high.astype(F32)).astype(BF16)


def thirds(x):
    high = x.astype(BF16)
    rest = x - high.astype(F32)
    mid = rest.astype(BF16)
    return high, mid, (rest - mid.astype(F32)).astype(BF16)


def dot(a, b):
    return jnp.dot(a, b, preferred_element_type=F32)


def dot_nt(a, b):
    return lax.dot_general(a, b, (((1,), (1,)), ((), ())), preferred_element_type=F32)


def wide_dot(wide, exact):
    return sum(dot(part, exact) for part in thirds(wide))


def dot_wide(exact, wide):
    return sum(dot(exact, part) for part in thirds(wide))


def restrict_kernel(
    side, probes, sources, table_xy, table_z, own, to_core, to_chip,
    rows, held, raw, fields, weights_xy, weights_z, arrived, ready,
):
    edges, fine_z = weights_xy.shape[0] // 2, rows.shape[1]
    cells = weights_xy.shape[1] // 2
    all_rows = own.shape[0]
    chunks = arrived.shape[0]
    share = held.shape[0] // chunks
    ranks = share // (2 * cells)
    groups = sources.shape[0]

    def arrival(i):
        part = pl.ds(i * share, share)
        return pltpu.make_async_copy(probes.at[part], held.at[part], arrived.at[i])

    small = [
        pltpu.make_async_copy(source, target, ready.at[i])
        for i, (source, target) in enumerate(
            ((sources, raw), (table_xy, weights_xy), (table_z, weights_z))
        )
    ]
    small[0].start()
    small[1].start()
    for i in range(chunks):
        arrival(i).start()
    small[2].start()
    small[0].wait()
    small[1].wait()
    fields[...] = raw[...].astype(F32)
    for i in range(chunks):
        g = i * groups // chunks
        arrival(i).wait()
        for pair in range(ranks // 2):
            first, second = (i * ranks + 2 * pair + k for k in range(2))
            high, low = ([], []), ([], [])
            for c in range(0, cells, 16):
                field0, field1 = fields[g, c : c + 16], fields[g, cells + c : cells + c + 16]
                for k, rank in enumerate((first, second)):
                    at = rank * 2 * cells + c
                    image = held[at : at + 16].astype(F32) * field0
                    image = image + held[at + cells : at + cells + 16].astype(F32) * field1
                    parts = halves(image)
                    high[k].append(parts[0])
                    low[k].append(parts[1])
            both = jnp.concatenate(
                [jnp.concatenate(high[k] + low[k], axis=0) for k in range(2)], axis=1
            )
            both = dot(weights_xy[...], both)
            both = both[:edges] + both[edges:]
            for k, rank in enumerate((first, second)):
                rows[rank * edges : (rank + 1) * edges, :] = both[:, k * fine_z : (k + 1) * fine_z]
    small[2].wait()
    per = weights_z.shape[0] // fine_z
    lanes = weights_z.shape[1] // 2
    layers = []
    for j in range(edges // per):
        total = 0.0
        for r in range(per):
            weights = weights_z[r * fine_z : (r + 1) * fine_z]
            for part in halves(rows[pl.ds(j * per + r, all_rows, stride=edges), :]):
                total = total + dot(part, weights)
        layers.append(total[:, :lanes] + total[:, lanes:])
    own[...] = jnp.concatenate(layers[1:-1], axis=1)
    odd = side[0] == 1
    to_core[...] = jnp.where(odd, layers[0], layers[-1])
    to_chip[...] = jnp.where(odd, layers[-1], layers[0])


def restrict(probes, sources, side):
    groups, ranks, steps_t, fine_x, fine_y, fine_z = probes.shape
    cells = fine_x * fine_y
    coarse_x, coarse_y, coarse_z = fine_x // 4, fine_y // 4, fine_z // 4
    edges_x = coarse_x + 4
    weights_x = spline_weights(fine_x, edges_x, -2)
    weights_y = spline_weights(fine_y, coarse_y, 0)
    weights_z = spline_weights(fine_z, coarse_z, 0)
    table_xy = np.einsum("xe,yd->edxy", weights_x, weights_y).reshape(edges_x * coarse_y, cells)
    high, low = two_terms(table_xy)
    table_xy = jnp.concatenate(
        [jnp.concatenate([high, high], axis=1), jnp.concatenate([low, low], axis=1)], axis=0
    )
    per = 128 // coarse_z
    table_z = np.einsum("zc,rs->rzsc", weights_z, np.eye(per)).reshape(per * fine_z, 128)
    table_z = jnp.concatenate(two_terms(table_z), axis=1)
    all_rows = groups * ranks
    lanes = edges_x * coarse_y * coarse_z - 256
    chunks = 2 * groups
    anywhere = pl.BlockSpec(memory_space=pl.ANY)
    vmem = pl.BlockSpec(memory_space=pltpu.VMEM)
    series = steps_t * cells
    return pl.pallas_call(
        restrict_kernel,
        in_specs=[pl.BlockSpec(memory_space=pltpu.SMEM)] + [anywhere] * 4,
        out_specs=[vmem] * 3,
        out_shape=[jax.ShapeDtypeStruct((all_rows, n), F32) for n in (lanes, 128, 128)],
        scratch_shapes=[
            pltpu.VMEM((edges_x * coarse_y * all_rows, fine_z), F32),
            pltpu.VMEM((all_rows * series, fine_z), BF16),
            pltpu.VMEM((groups, series, fine_z), BF16),
            pltpu.VMEM((groups, series, fine_z), F32),
            pltpu.VMEM(table_xy.shape, BF16),
            pltpu.VMEM(table_z.shape, BF16),
            pltpu.SemaphoreType.DMA((chunks,)),
            pltpu.SemaphoreType.DMA((3,)),
        ],
        compiler_params=pltpu.CompilerParams(vmem_limit_bytes=FULL_VMEM),
        name="restrict",
    )(
        side,
        probes.reshape(all_rows * series, fine_z),
        sources.reshape(groups, series, fine_z),
        table_xy,
        table_z,
    )


def products_kernel(ranks, place, *refs):
    *leaves, sketch, chosen, keep, send, keep_far, send_far, table = refs
    rows = leaves[0].shape[0]
    for i, leaf in enumerate(leaves):
        table[i * rows : (i + 1) * rows, :] = leaf[...]
    picked = chosen.shape[0] // ranks
    for i in range(picked):
        at = pl.multiple_of(place[i] * ranks, ranks)
        chosen[i * ranks : (i + 1) * ranks, :] = table[pl.ds(at, ranks), :]
    pieces = chosen[...]
    gram = dot_nt(pieces, pieces)
    cross = dot_nt(pieces, sketch[...])
    block = lambda i, j: gram[i * ranks : (i + 1) * ranks, j * ranks : (j + 1) * ranks]
    row = lambda *xs: jnp.concatenate(xs, axis=1)
    column = lambda *xs: jnp.concatenate(xs, axis=0)
    solo = lambda i: row(block(i, i), cross[i * ranks : (i + 1) * ranks])
    half = ranks // 2
    fold = lambda x: row(x[:half], x[half:])
    near = [column(solo(0), solo(1)), column(solo(2), solo(3))]
    far = [
        column(row(block(0, 2), block(0, 3)), fold(block(0, 1))),
        column(row(block(1, 2), block(1, 3)), fold(block(2, 3))),
    ]
    low = place[picked] == 0
    keep[...] = jnp.where(low, near[0], near[1])
    send[...] = jnp.where(low, near[1], near[0])
    keep_far[...] = jnp.where(low, far[0], far[1])
    send_far[...] = jnp.where(low, far[1], far[0])


def products(leaves, sketch, place, ranks):
    rows, lanes = leaves[0].shape
    count = len(leaves)
    half = (count * rows // ranks // 2) * ranks
    vmem = pl.BlockSpec(memory_space=pltpu.VMEM)
    near = jax.ShapeDtypeStruct((2 * ranks, 2 * ranks), F32)
    far = jax.ShapeDtypeStruct((3 * ranks // 2, 2 * ranks), F32)
    return pl.pallas_call(
        lambda *refs: products_kernel(ranks, *refs),
        in_specs=[pl.BlockSpec(memory_space=pltpu.SMEM)] + [vmem] * (count + 1),
        out_specs=[vmem] * 5,
        out_shape=[jax.ShapeDtypeStruct((half, lanes), BF16), near, near, far, far],
        scratch_shapes=[pltpu.VMEM((count * rows, lanes), BF16)],
        compiler_params=pltpu.CompilerParams(vmem_limit_bytes=VMEM_BYTES),
        name="products",
    )(place, *leaves, sketch)


def ridge_solve(systems):
    size = systems[0].shape[0]
    blocks = size // 8
    shape = (size, 2 * size)
    eye = lax.broadcasted_iota(jnp.int32, shape, 0) == lax.broadcasted_iota(jnp.int32, shape, 1)
    start = []
    for system in systems:
        trace = jnp.sum(jnp.where(eye, system, 0.0))
        system = system + jnp.where(eye, 0.01 * trace / size + 1e-06, 0.0)
        start.append(tuple(system[8 * i : 8 * i + 8] for i in range(blocks)))
    sub = lax.broadcasted_iota(jnp.int32, (8, 2 * size), 0)

    def eliminate(_, mats):
        done = []
        for mat in mats:
            head = mat[0]
            columns = [jnp.broadcast_to(head[:, j : j + 1], head.shape) for j in range(8)]
            for j in range(8):
                inverse = 1.0 / columns[j][j : j + 1]
                here = sub == j
                row = head[j : j + 1] * inverse
                head = jnp.where(here, row, head - columns[j] * row)
                for m in range(j + 1, 8):
                    entry = columns[m][j : j + 1] * inverse
                    columns[m] = jnp.where(here, entry, columns[m] - columns[j] * entry)
            rest = []
            for block in mat[1:]:
                new = block
                for j in range(8):
                    new = new - block[:, j : j + 1] * head[j : j + 1]
                rest.append(new)
            done.append(tuple(pltpu.roll(x, 2 * size - 8, 1) for x in rest + [head]))
        return tuple(done)

    mats = lax.fori_loop(0, blocks, eliminate, tuple(start))
    return [jnp.concatenate(mat, axis=0)[:, :size].astype(BF16) for mat in mats]


def flip(x):
    return x.astype(F32).T.astype(BF16)


def leaf_kernel(near, coefs):
    size = near.shape[0] // 2
    a, b = ridge_solve([near[:size], near[size:]])
    coefs[:size, :] = a
    coefs[size:, :] = b


def pair_kernel(scaling, near, far, coefs, out):
    size = near.shape[0] // 2
    half = size // 2
    row = lambda *xs: jnp.concatenate(xs, axis=1)
    column = lambda *xs: jnp.concatenate(xs, axis=0)
    corner = column(far[size:, :size], far[size:, size:])
    joint = column(row(near[:size, :size], corner), row(corner.T, near[size:, :size]))
    cross = column(near[:size, size:], near[size:, size:])
    both = coefs[...]
    both_t = flip(both)
    gram = scaling * scaling * dot_wide(both_t, wide_dot(joint, both))
    system = row(gram, scaling * dot_wide(both_t, cross))
    (own,) = ridge_solve([system])
    out[:size, :] = system
    out[size : 2 * size, :] = far[:size, :]
    out[2 * size : 3 * size, :] = row(both[:size], both[size:]).astype(F32)
    out[3 * size :, :] = row(own[:half], own[half:]).astype(F32)


def root_kernel(scaling, place, mine, other, pieces, own, send, table):
    size = mine.shape[1] // 2
    half = size // 2
    row = lambda *xs: jnp.concatenate(xs, axis=1)
    column = lambda *xs: jnp.concatenate(xs, axis=0)
    low = place[0] == 0
    p = jnp.where(low, mine[...], other[...])
    q = jnp.where(low, other[...], mine[...])
    corner = column(p[size : 2 * size], q[size : 2 * size])
    coefs = [x[2 * size : 3 * size].astype(BF16) for x in (p, q)]
    coefs = [column(x[:, :size], x[:, size:]) for x in coefs]
    coefs_t = [flip(x) for x in coefs]
    tops = [x[3 * size :].astype(BF16) for x in (p, q)]
    tops = [column(x[:, :size], x[:, size:]) for x in tops]
    tops_t = [flip(x) for x in tops]
    square = scaling * scaling
    corner = square * dot_wide(coefs_t[0], wide_dot(corner, coefs[1]))
    joint = column(row(p[:size, :size], corner), row(corner.T, q[:size, :size]))
    both, both_t = column(*tops), row(*tops_t)
    gram = square * dot_wide(both_t, wide_dot(joint, both))
    cross = scaling * dot_wide(both_t, column(p[:size, size:], q[:size, size:]))
    (last,) = ridge_solve([row(gram, cross)])
    last_t = flip(last)
    total_t = row(*(wide_dot(dot(last_t, t), c) for t, c in zip(tops_t, coefs_t)))
    result = (square * scaling) * sum(dot(part, pieces[...]) for part in halves(total_t))
    table[:size, :] = result[:, : 2 * size]
    table[size:, :] = result[:, 2 * size :]
    count = own.shape[0]
    for out, at in ((own, place[1]), (send, place[2])):
        at = pl.multiple_of(at * count, count)
        for i in range(2):
            out[:, i * 2 * size : (i + 1) * 2 * size] = table[pl.ds(at + i * size, count), :]


def local_call(kernel, name, out, *args, scalars=(), scratch=(), flops=1 << 24):
    vmem = pl.BlockSpec(memory_space=pltpu.VMEM)
    smem = pl.BlockSpec(memory_space=pltpu.SMEM)
    return pl.pallas_call(
        kernel,
        in_specs=[smem] * len(scalars) + [vmem] * len(args),
        out_specs=jax.tree.map(lambda _: vmem, out),
        out_shape=out,
        scratch_shapes=scratch,
        compiler_params=pltpu.CompilerParams(vmem_limit_bytes=VMEM_BYTES),
        cost_estimate=pl.CostEstimate(flops=flops, bytes_accessed=1 << 17, transcendentals=0),
        name=name,
    )(*scalars, *args)


def swap(x, axis, mask):
    return lax.ppermute(x, axis, [(i, i ^ mask) for i in range(lax.axis_size(axis))])


def body(probes, sources, sketch, pairing):
    groups, ranks = probes.shape[:2]
    coarse_x = probes.shape[3] // 4
    layer = sketch.shape[2]
    shots, space = lax.axis_size("shots"), lax.axis_size("space")
    shot, place = lax.axis_index("shots"), lax.axis_index("space")
    scaling = math.sqrt(coarse_x * space * layer / ranks)
    side = place % 2

    own, to_core, to_chip = restrict(probes, sources, side[None].astype(jnp.int32))
    from_core = swap(to_core, "space", 1)
    across = [(i, i + 1 if i % 2 else i - 1) for i in range(space)]
    from_chip = lax.ppermute(to_chip, "space", [(i, j) for i, j in across if 0 <= j < space])
    from_below = jnp.where(side == 0, from_chip, from_core)
    from_above = jnp.where(side == 0, from_core, from_chip)
    leaf = (own + jnp.concatenate([from_below, from_above], axis=1)).astype(BF16)

    leaves = [leaf] + [swap(leaf, "shots", m) for m in range(1, shots)]
    picked = shots * groups // 2
    chosen = lax.dynamic_slice_in_dim(pairing, shot // (shots // 2) * picked, picked)
    slots = (chosen // groups ^ shot) * groups + chosen % groups
    sketch_t = jnp.transpose(sketch, (1, 0, 2)).reshape(ranks, coarse_x * layer)
    slots = jnp.concatenate([slots, side[None]]).astype(jnp.int32)
    pieces, near, send, far, send_far = products(leaves, sketch_t, slots, ranks)

    near = near + swap(send, "space", 1)
    far = far + swap(send_far, "space", 1)
    mask = 2
    while mask < space:
        near = near + swap(near, "space", mask)
        far = far + swap(far, "space", mask)
        mask *= 2
    coefs = local_call(
        leaf_kernel, "leaf_coefs", jax.ShapeDtypeStruct((2 * ranks, ranks), BF16), near,
        flops=1 << 32,
    )
    mine = local_call(
        lambda *refs: pair_kernel(scaling, *refs), "pair",
        jax.ShapeDtypeStruct((7 * ranks // 2, 2 * ranks), F32), near, far, coefs,
    )
    other = swap(mine, "space", 1)

    columns = ranks // shots
    across_tree = shots // 2
    spots = jnp.stack([side, shot, shot ^ across_tree]).astype(jnp.int32)
    part = jax.ShapeDtypeStruct((columns, pieces.shape[1]), F32)
    own_part, sent = local_call(
        lambda *refs: root_kernel(scaling, *refs), "root", [part, part], mine, other, pieces,
        scalars=(spots,), scratch=[pltpu.VMEM((2 * ranks, 2 * ranks), F32)],
    )
    total = (own_part + swap(sent, "shots", across_tree)).astype(BF16)
    return jnp.transpose(total.reshape(columns, coarse_x, layer), (1, 0, 2))


def solution(mesh):
    in_specs = (
        P("shots", None, None, "space", None, None),
        P("shots", None, "space", None, None),
        P("space", None, None),
        P(),
    )
    out_specs = P("space", "shots", None)
    return jax.shard_map(body, mesh=mesh, in_specs=in_specs, out_specs=out_specs, check_vma=False)
```

```python
import math

import jax
import jax.numpy as jnp
import numpy as np
from jax import lax
from jax.experimental import pallas as pl
from jax.experimental.pallas import tpu as pltpu
from jax.sharding import PartitionSpec as P

F32 = jnp.float32
BF16 = jnp.bfloat16
VMEM_BYTES = 48 << 20
FRONT_VMEM = 24 << 20


def spline_weights(fine_count, coarse_count, coarse_start):
    fine = np.arange(fine_count, dtype=np.float64)
    coarse = np.arange(coarse_count, dtype=np.float64) + coarse_start
    s = np.abs((fine[:, None] + 0.5 - 4.0 * coarse[None, :] - 2.0) / 4.0)
    inner = 2.0 / 3.0 - s**2 + 0.5 * s**3
    outer = np.maximum(2.0 - s, 0.0) ** 3 / 6.0
    return np.where(s < 1.0, inner, outer) / 4.0


def two_terms(table):
    table = jnp.asarray(table, F32)
    high = table.astype(BF16)
    return high, (table - high.astype(F32)).astype(BF16)


def halves(x):
    high = x.astype(BF16)
    return high, (x - high.astype(F32)).astype(BF16)


def thirds(x):
    high = x.astype(BF16)
    rest = x - high.astype(F32)
    mid = rest.astype(BF16)
    return high, mid, (rest - mid.astype(F32)).astype(BF16)


def dot(a, b):
    return jnp.dot(a, b, preferred_element_type=F32)


def dot_nt(a, b):
    return lax.dot_general(a, b, (((1,), (1,)), ((), ())), preferred_element_type=F32)


def wide_dot(wide, exact):
    return sum(dot(part, exact) for part in thirds(wide))


def dot_wide(exact, wide):
    return sum(dot(exact, part) for part in thirds(wide))


def restrict_kernel(
    side, probes, sources, table_xy, table_z, own, to_core, to_chip,
    rows, held, raw, fields, weights_xy, weights_z, arrived, ready,
):
    edges, fine_z = weights_xy.shape[0] // 2, rows.shape[1]
    cells = weights_xy.shape[1] // 2
    all_rows = own.shape[0]
    chunks = arrived.shape[0]
    share = held.shape[0] // chunks
    ranks = share // (2 * cells)
    groups = sources.shape[0]

    def arrival(i):
        part = pl.ds(i * share, share)
        return pltpu.make_async_copy(probes.at[part], held.at[part], arrived.at[i])

    small = [
        pltpu.make_async_copy(source, target, ready.at[i])
        for i, (source, target) in enumerate(
            ((sources, raw), (table_xy, weights_xy), (table_z, weights_z))
        )
    ]
    small[0].start()
    small[1].start()
    for i in range(chunks):
        arrival(i).start()
    small[2].start()
    small[0].wait()
    small[1].wait()
    fields[...] = raw[...].astype(F32)
    for i in range(chunks):
        g = i * groups // chunks
        arrival(i).wait()
        for pair in range(ranks // 2):
            first, second = (i * ranks + 2 * pair + k for k in range(2))
            high, low = ([], []), ([], [])
            for c in range(0, cells, 16):
                field0, field1 = fields[g, c : c + 16], fields[g, cells + c : cells + c + 16]
                for k, rank in enumerate((first, second)):
                    at = rank * 2 * cells + c
                    image = held[at : at + 16].astype(F32) * field0
                    image = image + held[at + cells : at + cells + 16].astype(F32) * field1
                    parts = halves(image)
                    high[k].append(parts[0])
                    low[k].append(parts[1])
            both = jnp.concatenate(
                [jnp.concatenate(high[k] + low[k], axis=0) for k in range(2)], axis=1
            )
            both = dot(weights_xy[...], both)
            both = both[:edges] + both[edges:]
            for k, rank in enumerate((first, second)):
                rows[rank * edges : (rank + 1) * edges, :] = both[:, k * fine_z : (k + 1) * fine_z]
    small[2].wait()
    per = weights_z.shape[0] // fine_z
    lanes = weights_z.shape[1] // 2
    layers = []
    for j in range(edges // per):
        total = 0.0
        for r in range(per):
            weights = weights_z[r * fine_z : (r + 1) * fine_z]
            for part in halves(rows[pl.ds(j * per + r, all_rows, stride=edges), :]):
                total = total + dot(part, weights)
        layers.append(total[:, :lanes] + total[:, lanes:])
    own[...] = jnp.concatenate(layers[1:-1], axis=1)
    odd = side[0] == 1
    to_core[...] = jnp.where(odd, layers[0], layers[-1])
    to_chip[...] = jnp.where(odd, layers[-1], layers[0])


def restrict(probes, sources, side):
    groups, ranks, steps_t, fine_x, fine_y, fine_z = probes.shape
    cells = fine_x * fine_y
    coarse_x, coarse_y, coarse_z = fine_x // 4, fine_y // 4, fine_z // 4
    edges_x = coarse_x + 4
    weights_x = spline_weights(fine_x, edges_x, -2)
    weights_y = spline_weights(fine_y, coarse_y, 0)
    weights_z = spline_weights(fine_z, coarse_z, 0)
    table_xy = np.einsum("xe,yd->edxy", weights_x, weights_y).reshape(edges_x * coarse_y, cells)
    high, low = two_terms(table_xy)
    table_xy = jnp.concatenate(
        [jnp.concatenate([high, high], axis=1), jnp.concatenate([low, low], axis=1)], axis=0
    )
    per = 128 // coarse_z
    table_z = np.einsum("zc,rs->rzsc", weights_z, np.eye(per)).reshape(per * fine_z, 128)
    table_z = jnp.concatenate(two_terms(table_z), axis=1)
    all_rows = groups * ranks
    lanes = edges_x * coarse_y * coarse_z - 256
    chunks = 2 * groups
    outside = pl.BlockSpec(memory_space=pltpu.HBM)
    vmem = pl.BlockSpec(memory_space=pltpu.VMEM)
    series = steps_t * cells
    return pl.pallas_call(
        restrict_kernel,
        in_specs=[pl.BlockSpec(memory_space=pltpu.SMEM)] + [outside] * 4,
        out_specs=[vmem] * 3,
        out_shape=[pltpu.VMEM((all_rows, n), F32) for n in (lanes, 128, 128)],
        scratch_shapes=[
            pltpu.VMEM((edges_x * coarse_y * all_rows, fine_z), F32),
            pltpu.VMEM((all_rows * series, fine_z), BF16),
            pltpu.VMEM((groups, series, fine_z), BF16),
            pltpu.VMEM((groups, series, fine_z), F32),
            pltpu.VMEM(table_xy.shape, BF16),
            pltpu.VMEM(table_z.shape, BF16),
            pltpu.SemaphoreType.DMA((chunks,)),
            pltpu.SemaphoreType.DMA((3,)),
        ],
        compiler_params=pltpu.CompilerParams(vmem_limit_bytes=FRONT_VMEM),
        name="restrict",
    )(
        side,
        *(
            pltpu.with_memory_space_constraint(x, pltpu.HBM)
            for x in (
                probes.reshape(all_rows * series, fine_z),
                sources.reshape(groups, series, fine_z),
                table_xy,
                table_z,
            )
        ),
    )


def products_kernel(ranks, place, *refs):
    *leaves, sketch, chosen, keep, send, keep_far, send_far, table = refs
    rows = leaves[0].shape[0]
    for i, leaf in enumerate(leaves):
        table[i * rows : (i + 1) * rows, :] = leaf[...]
    picked = chosen.shape[0] // ranks
    for i in range(picked):
        at = pl.multiple_of(place[i] * ranks, ranks)
        chosen[i * ranks : (i + 1) * ranks, :] = table[pl.ds(at, ranks), :]
    pieces = chosen[...]
    gram = dot_nt(pieces, pieces)
    cross = dot_nt(pieces, sketch[...])
    block = lambda i, j: gram[i * ranks : (i + 1) * ranks, j * ranks : (j + 1) * ranks]
    row = lambda *xs: jnp.concatenate(xs, axis=1)
    column = lambda *xs: jnp.concatenate(xs, axis=0)
    solo = lambda i: row(block(i, i), cross[i * ranks : (i + 1) * ranks])
    half = ranks // 2
    fold = lambda x: row(x[:half], x[half:])
    near = [column(solo(i), solo(i + 1)) for i in (0, 2)]
    far = [column(fold(block(2 * i, 2 * i + 1)), row(block(i, 2), block(i, 3))) for i in (0, 1)]
    low = place[picked] == 0
    keep[...] = jnp.where(low, near[0], near[1])
    send[...] = jnp.where(low, near[1], near[0])
    keep_far[...] = jnp.where(low, far[0], far[1])
    send_far[...] = jnp.where(low, far[1], far[0])


def products(leaves, sketch, place, ranks):
    rows, lanes = leaves[0].shape
    count = len(leaves)
    half = (count * rows // ranks // 2) * ranks
    vmem = pl.BlockSpec(memory_space=pltpu.VMEM)
    near = jax.ShapeDtypeStruct((2 * ranks, 2 * ranks), F32)
    far = jax.ShapeDtypeStruct((3 * ranks // 2, 2 * ranks), F32)
    return pl.pallas_call(
        lambda *refs: products_kernel(ranks, *refs),
        in_specs=[pl.BlockSpec(memory_space=pltpu.SMEM)] + [vmem] * (count + 1),
        out_specs=[vmem] * 5,
        out_shape=[jax.ShapeDtypeStruct((half, lanes), BF16), near, near, far, far],
        scratch_shapes=[pltpu.VMEM((count * rows, lanes), BF16)],
        compiler_params=pltpu.CompilerParams(vmem_limit_bytes=VMEM_BYTES),
        name="products",
    )(place, *leaves, sketch)


def ridge_solve(systems):
    size = systems[0].shape[0]
    blocks = size // 8
    shape = (size, 2 * size)
    eye = lax.broadcasted_iota(jnp.int32, shape, 0) == lax.broadcasted_iota(jnp.int32, shape, 1)
    mats = []
    for system in systems:
        trace = jnp.sum(jnp.where(eye, system, 0.0))
        system = system + jnp.where(eye, 0.01 * trace / size + 1e-06, 0.0)
        mats.append([system[8 * i : 8 * i + 8] for i in range(blocks)])
    sub = lax.broadcasted_iota(jnp.int32, (8, 2 * size), 0)
    for k in range(blocks):
        lane = 8 * k
        for mat in mats:
            head = mat[k]
            columns = [
                jnp.broadcast_to(head[:, lane + j : lane + j + 1], head.shape) for j in range(8)
            ]
            for j in range(0, 8, 2):
                left, right = columns[j], columns[j + 1]
                a, b, c = left[j : j + 1], left[j + 1 : j + 2], right[j + 1 : j + 2]
                inverse = 1.0 / (a * c - b * b)

                def reduced(x):
                    p, q = x[j : j + 1], x[j + 1 : j + 2]
                    p, q = (c * p - b * q) * inverse, (a * q - b * p) * inverse
                    rest = (x - left * p) - right * q
                    return jnp.where(sub == j, p, jnp.where(sub == j + 1, q, rest))

                head = reduced(head)
                for m in range(j + 2, 8):
                    columns[m] = reduced(columns[m])
            for i in range(blocks):
                if i != k:
                    new = mat[i]
                    for j in range(8):
                        new = new - mat[i][:, lane + j : lane + j + 1] * head[j : j + 1]
                    mat[i] = new
            mat[k] = head
    return [jnp.concatenate(mat, axis=0)[:, size:].astype(BF16) for mat in mats]


def flip(x):
    return x.astype(F32).T.astype(BF16)


def pair_kernel(scaling, near, far, out):
    size = near.shape[1] // 2
    half = size // 2
    row = lambda *xs: jnp.concatenate(xs, axis=1)
    column = lambda *xs: jnp.concatenate(xs, axis=0)
    corner = column(far[:half, :size], far[:half, size:])
    joint = column(row(near[:size, :size], corner), row(corner.T, near[size:, :size]))
    cross = column(near[:size, size:], near[size:, size:])
    both = column(*ridge_solve([near[:size], near[size:]]))
    both_t = flip(both)
    gram = scaling * scaling * dot_wide(both_t, wide_dot(joint, both))
    system = row(gram, scaling * dot_wide(both_t, cross))
    (own,) = ridge_solve([system])
    out[:size, :] = system
    out[size : 2 * size, :] = dot(flip(own), both_t)
    out[2 * size : 2 * size + half, :] = row(own[:half], own[half:]).astype(F32)
    out[2 * size + half :, :] = far[half:, :]


def root_kernel(scaling, place, mine, other, pieces, own, send, table):
    size = mine.shape[1] // 2
    row = lambda *xs: jnp.concatenate(xs, axis=1)
    column = lambda *xs: jnp.concatenate(xs, axis=0)
    low = place[0] == 0
    a, b = mine[size : 2 * size, :], other[size : 2 * size, :]
    p, q = jnp.where(low, a, b), jnp.where(low, b, a)
    last = 5 * size // 2
    a, b = mine[last:, :], other[last:, :]
    corner = column(jnp.where(low, a, b), jnp.where(low, b, a))
    square = scaling * scaling
    exact = dict(precision=lax.Precision.HIGHEST, preferred_element_type=F32)
    right = lax.dot_general(corner, q, (((1,), (1,)), ((), ())), **exact)
    across = (square * square) * jnp.dot(p, right, **exact)
    gram, cross = across + across.T, 0.0
    for half in (mine, other):
        coef = half[2 * size : last, :].astype(BF16)
        coef = column(coef[:, :size], coef[:, size:])
        coef_t = flip(coef)
        gram = gram + square * dot_wide(coef_t, wide_dot(half[:size, :size], coef))
        cross = cross + scaling * dot_wide(coef_t, half[:size, size:])
    (last,) = ridge_solve([row(gram, cross)])
    total_t = dot_wide(flip(last), row(p, q))
    result = (square * scaling) * sum(dot(part, pieces[...]) for part in halves(total_t))
    table[:size, :] = result[:, : 2 * size]
    table[size:, :] = result[:, 2 * size :]
    count = own.shape[0]
    for out, at in ((own, place[1]), (send, place[2])):
        at = pl.multiple_of(at * count, count)
        for i in range(2):
            out[:, i * 2 * size : (i + 1) * 2 * size] = table[pl.ds(at + i * size, count), :]


def local_call(kernel, name, out, *args, scalars=(), scratch=(), flops=1 << 24):
    vmem = pl.BlockSpec(memory_space=pltpu.VMEM)
    smem = pl.BlockSpec(memory_space=pltpu.SMEM)
    return pl.pallas_call(
        kernel,
        in_specs=[smem] * len(scalars) + [vmem] * len(args),
        out_specs=jax.tree.map(lambda _: vmem, out),
        out_shape=out,
        scratch_shapes=scratch,
        compiler_params=pltpu.CompilerParams(vmem_limit_bytes=VMEM_BYTES),
        cost_estimate=pl.CostEstimate(flops=flops, bytes_accessed=1 << 17, transcendentals=0),
        name=name,
    )(*scalars, *args)


def swap(x, axis, mask):
    return lax.ppermute(x, axis, [(i, i ^ mask) for i in range(lax.axis_size(axis))])


def body(probes, sources, sketch, pairing):
    groups, ranks = probes.shape[:2]
    coarse_x = probes.shape[3] // 4
    layer = sketch.shape[2]
    shots, space = lax.axis_size("shots"), lax.axis_size("space")
    shot, place = lax.axis_index("shots"), lax.axis_index("space")
    scaling = math.sqrt(coarse_x * space * layer / ranks)
    side = place % 2

    own, to_core, to_chip = restrict(probes, sources, side[None].astype(jnp.int32))
    from_core = swap(to_core, "space", 1)
    across = [(i, (i + 1 if i % 2 else i - 1) % space) for i in range(space)]
    from_chip = lax.ppermute(to_chip, "space", across)
    from_chip = jnp.where((place == 0) | (place == space - 1), 0.0, from_chip)
    from_below = jnp.where(side == 0, from_chip, from_core)
    from_above = jnp.where(side == 0, from_core, from_chip)
    leaf = (own + jnp.concatenate([from_below, from_above], axis=1)).astype(BF16)

    leaves = [leaf] + [swap(leaf, "shots", m) for m in range(1, shots)]
    picked = shots * groups // 2
    chosen = lax.dynamic_slice_in_dim(pairing, shot // (shots // 2) * picked, picked)
    slots = (chosen // groups ^ shot) * groups + chosen % groups
    sketch_t = jnp.transpose(sketch, (1, 0, 2)).reshape(ranks, coarse_x * layer)
    slots = jnp.concatenate([slots, side[None]]).astype(jnp.int32)
    pieces, near, send, far, send_far = products(leaves, sketch_t, slots, ranks)

    near = near + swap(send, "space", 1)
    far = far + swap(send_far, "space", 1)
    mask = 2
    while mask < space:
        near, far = near + swap(near, "space", mask), far + swap(far, "space", mask)
        mask *= 2
    mine = local_call(
        lambda *refs: pair_kernel(scaling, *refs), "pair",
        jax.ShapeDtypeStruct((7 * ranks // 2, 2 * ranks), F32), near, far,
    )
    other = swap(mine, "space", 1)

    columns = ranks // shots
    across_tree = shots // 2
    spots = jnp.stack([side, shot, shot ^ across_tree]).astype(jnp.int32)
    part = jax.ShapeDtypeStruct((columns, pieces.shape[1]), F32)
    own_part, sent = local_call(
        lambda *refs: root_kernel(scaling, *refs), "root", [part, part], mine, other, pieces,
        scalars=(spots,), scratch=[pltpu.VMEM((2 * ranks, 2 * ranks), F32)],
    )
    total = (own_part + swap(sent, "shots", across_tree)).astype(BF16)
    return jnp.transpose(total.reshape(columns, coarse_x, layer), (1, 0, 2))


def solution(mesh):
    in_specs = (
        P("shots", None, None, "space", None, None),
        P("shots", None, "space", None, None),
        P("space", None, None),
        P(),
    )
    out_specs = P("space", "shots", None)
    return jax.shard_map(body, mesh=mesh, in_specs=in_specs, out_specs=out_specs, check_vma=False)
```

```python
import math

import jax
import jax.numpy as jnp
import numpy as np
from jax import lax
from jax.experimental import pallas as pl
from jax.experimental.pallas import tpu as pltpu
from jax.sharding import PartitionSpec as P

F32 = jnp.float32
BF16 = jnp.bfloat16
VMEM_BYTES = 48 << 20
FRONT_VMEM = 24 << 20


def spline_weights(fine_count, coarse_count, coarse_start):
    fine = np.arange(fine_count, dtype=np.float64)
    coarse = np.arange(coarse_count, dtype=np.float64) + coarse_start
    s = np.abs((fine[:, None] + 0.5 - 4.0 * coarse[None, :] - 2.0) / 4.0)
    inner = 2.0 / 3.0 - s**2 + 0.5 * s**3
    outer = np.maximum(2.0 - s, 0.0) ** 3 / 6.0
    return np.where(s < 1.0, inner, outer) / 4.0


def two_terms(table):
    table = jnp.asarray(table, F32)
    high = table.astype(BF16)
    return high, (table - high.astype(F32)).astype(BF16)


def halves(x):
    high = x.astype(BF16)
    return high, (x - high.astype(F32)).astype(BF16)


def thirds(x):
    high = x.astype(BF16)
    rest = x - high.astype(F32)
    mid = rest.astype(BF16)
    return high, mid, (rest - mid.astype(F32)).astype(BF16)


def dot(a, b):
    return jnp.dot(a, b, preferred_element_type=F32)


def dot_nt(a, b):
    return lax.dot_general(a, b, (((1,), (1,)), ((), ())), preferred_element_type=F32)


def wide_dot(wide, exact):
    return sum(dot(part, exact) for part in thirds(wide))


def dot_wide(exact, wide):
    return sum(dot(exact, part) for part in thirds(wide))


def restrict_kernel(
    side, probes, sources, table_xy, table_z, own, to_core, to_chip,
    rows, held, raw, fields, weights_xy, weights_z, arrived, ready,
):
    edges, fine_z = weights_xy.shape[0] // 2, rows.shape[1]
    cells = weights_xy.shape[1] // 2
    all_rows = own.shape[0]
    chunks = arrived.shape[0]
    share = held.shape[0] // chunks
    ranks = share // (2 * cells)
    groups = sources.shape[0]

    def arrival(i):
        part = pl.ds(i * share, share)
        return pltpu.make_async_copy(probes.at[part], held.at[part], arrived.at[i])

    small = [
        pltpu.make_async_copy(source, target, ready.at[i])
        for i, (source, target) in enumerate(
            ((sources, raw), (table_xy, weights_xy), (table_z, weights_z))
        )
    ]
    small[0].start()
    small[1].start()
    ahead = chunks - 1
    for i in range(ahead):
        arrival(i).start()
    small[2].start()
    small[0].wait()
    small[1].wait()
    fields[...] = raw[...].astype(F32)
    for i in range(chunks):
        g = i * groups // chunks
        arrival(i).wait()
        if i + ahead < chunks:
            arrival(i + ahead).start()
        for pair in range(ranks // 2):
            first, second = (i * ranks + 2 * pair + k for k in range(2))
            high, low = ([], []), ([], [])
            for c in range(0, cells, 16):
                field0, field1 = fields[g, c : c + 16], fields[g, cells + c : cells + c + 16]
                for k, rank in enumerate((first, second)):
                    at = rank * 2 * cells + c
                    image = held[at : at + 16].astype(F32) * field0
                    image = image + held[at + cells : at + cells + 16].astype(F32) * field1
                    parts = halves(image)
                    high[k].append(parts[0])
                    low[k].append(parts[1])
            both = jnp.concatenate(
                [jnp.concatenate(high[k] + low[k], axis=0) for k in range(2)], axis=1
            )
            both = dot(weights_xy[...], both)
            both = both[:edges] + both[edges:]
            for k, rank in enumerate((first, second)):
                rows[rank * edges : (rank + 1) * edges, :] = both[:, k * fine_z : (k + 1) * fine_z]
    small[2].wait()
    per = weights_z.shape[0] // fine_z
    lanes = weights_z.shape[1] // 2
    layers = []
    for j in range(edges // per):
        parts = [halves(rows[pl.ds(j * per + r, all_rows, stride=edges), :]) for r in range(per)]
        total = sum(dot(jnp.concatenate(x, axis=1), weights_z[...]) for x in zip(*parts))
        layers.append(total[:, :lanes] + total[:, lanes:])
    own[...] = jnp.concatenate(layers[1:-1], axis=1)
    odd = side[0] == 1
    to_core[...] = jnp.where(odd, layers[0], layers[-1])
    to_chip[...] = jnp.where(odd, layers[-1], layers[0])


def restrict(probes, sources, side):
    groups, ranks, steps_t, fine_x, fine_y, fine_z = probes.shape
    cells = fine_x * fine_y
    coarse_x, coarse_y, coarse_z = fine_x // 4, fine_y // 4, fine_z // 4
    edges_x = coarse_x + 4
    weights_x = spline_weights(fine_x, edges_x, -2)
    weights_y = spline_weights(fine_y, coarse_y, 0)
    weights_z = spline_weights(fine_z, coarse_z, 0)
    table_xy = np.einsum("xe,yd->edxy", weights_x, weights_y).reshape(edges_x * coarse_y, cells)
    high, low = two_terms(table_xy)
    table_xy = jnp.concatenate(
        [jnp.concatenate([high, high], axis=1), jnp.concatenate([low, low], axis=1)], axis=0
    )
    per = 128 // coarse_z
    table_z = np.einsum("zc,rs->rzsc", weights_z, np.eye(per)).reshape(per * fine_z, 128)
    table_z = jnp.concatenate(two_terms(table_z), axis=1)
    all_rows = groups * ranks
    lanes = edges_x * coarse_y * coarse_z - 256
    chunks = 2 * groups
    outside = pl.BlockSpec(memory_space=pltpu.HBM)
    vmem = pl.BlockSpec(memory_space=pltpu.VMEM)
    series = steps_t * cells
    return pl.pallas_call(
        restrict_kernel,
        in_specs=[pl.BlockSpec(memory_space=pltpu.SMEM)] + [outside] * 4,
        out_specs=[vmem] * 3,
        out_shape=[pltpu.VMEM((all_rows, n), F32) for n in (lanes, 128, 128)],
        scratch_shapes=[
            pltpu.VMEM((edges_x * coarse_y * all_rows, fine_z), F32),
            pltpu.VMEM((all_rows * series, fine_z), BF16),
            pltpu.VMEM((groups, series, fine_z), BF16),
            pltpu.VMEM((groups, series, fine_z), F32),
            pltpu.VMEM(table_xy.shape, BF16),
            pltpu.VMEM(table_z.shape, BF16),
            pltpu.SemaphoreType.DMA((chunks,)),
            pltpu.SemaphoreType.DMA((3,)),
        ],
        compiler_params=pltpu.CompilerParams(vmem_limit_bytes=FRONT_VMEM),
        name="restrict",
    )(
        side,
        *(
            pltpu.with_memory_space_constraint(x, pltpu.HBM)
            for x in (
                probes.reshape(all_rows * series, fine_z),
                sources.reshape(groups, series, fine_z),
                table_xy,
                table_z,
            )
        ),
    )


def products_kernel(ranks, place, *refs):
    *leaves, sketch, chosen, keep, send, keep_far, send_far, table = refs
    rows = leaves[0].shape[0]
    for i, leaf in enumerate(leaves):
        table[i * rows : (i + 1) * rows, :] = leaf[...]
    picked = chosen.shape[0] // ranks
    for i in range(picked):
        at = pl.multiple_of(place[i] * ranks, ranks)
        chosen[i * ranks : (i + 1) * ranks, :] = table[pl.ds(at, ranks), :]
    pieces = chosen[...]
    gram = dot_nt(pieces, pieces)
    cross = dot_nt(pieces, sketch[...])
    block = lambda i, j: gram[i * ranks : (i + 1) * ranks, j * ranks : (j + 1) * ranks]
    row = lambda *xs: jnp.concatenate(xs, axis=1)
    column = lambda *xs: jnp.concatenate(xs, axis=0)
    solo = lambda i: row(block(i, i), cross[i * ranks : (i + 1) * ranks])
    half = ranks // 2
    fold = lambda x: row(x[:half], x[half:])
    near = [column(solo(i), solo(i + 1)) for i in (0, 2)]
    far = [column(fold(block(2 * i, 2 * i + 1)), row(block(i, 2), block(i, 3))) for i in (0, 1)]
    low = place[picked] == 0
    keep[...] = jnp.where(low, near[0], near[1])
    send[...] = jnp.where(low, near[1], near[0])
    keep_far[...] = jnp.where(low, far[0], far[1])
    send_far[...] = jnp.where(low, far[1], far[0])


def products(leaves, sketch, place, ranks):
    rows, lanes = leaves[0].shape
    count = len(leaves)
    half = (count * rows // ranks // 2) * ranks
    vmem = pl.BlockSpec(memory_space=pltpu.VMEM)
    near = jax.ShapeDtypeStruct((2 * ranks, 2 * ranks), F32)
    far = jax.ShapeDtypeStruct((3 * ranks // 2, 2 * ranks), F32)
    return pl.pallas_call(
        lambda *refs: products_kernel(ranks, *refs),
        in_specs=[pl.BlockSpec(memory_space=pltpu.SMEM)] + [vmem] * (count + 1),
        out_specs=[vmem] * 5,
        out_shape=[jax.ShapeDtypeStruct((half, lanes), BF16), near, near, far, far],
        scratch_shapes=[pltpu.VMEM((count * rows, lanes), BF16)],
        compiler_params=pltpu.CompilerParams(vmem_limit_bytes=VMEM_BYTES),
        name="products",
    )(place, *leaves, sketch)


def ridge_solve(systems):
    size = systems[0].shape[0]
    blocks = size // 8
    shape = (size, 2 * size)
    eye = lax.broadcasted_iota(jnp.int32, shape, 0) == lax.broadcasted_iota(jnp.int32, shape, 1)
    mats = []
    for system in systems:
        trace = jnp.sum(jnp.where(eye, system, 0.0))
        system = system + jnp.where(eye, 0.01 * trace / size + 1e-06, 0.0)
        mats.append([system[8 * i : 8 * i + 8] for i in range(blocks)])
    sub = lax.broadcasted_iota(jnp.int32, (8, 2 * size), 0)
    for k in range(blocks):
        lane = 8 * k
        for mat in mats:
            head = mat[k]
            columns = [
                jnp.broadcast_to(head[:, lane + j : lane + j + 1], head.shape) for j in range(8)
            ]
            for j in range(0, 8, 2):
                left, right = columns[j], columns[j + 1]
                a, b, c = left[j : j + 1], left[j + 1 : j + 2], right[j + 1 : j + 2]
                inverse = 1.0 / (a * c - b * b)

                def reduced(x):
                    p, q = x[j : j + 1], x[j + 1 : j + 2]
                    p, q = (c * p - b * q) * inverse, (a * q - b * p) * inverse
                    rest = (x - left * p) - right * q
                    return jnp.where(sub == j, p, jnp.where(sub == j + 1, q, rest))

                head = reduced(head)
                for m in range(j + 2, 8):
                    columns[m] = reduced(columns[m])
            for i in range(blocks):
                if i != k:
                    new = mat[i]
                    for j in range(8):
                        new = new - mat[i][:, lane + j : lane + j + 1] * head[j : j + 1]
                    mat[i] = new
            mat[k] = head
    return [jnp.concatenate(mat, axis=0)[:, size:].astype(BF16) for mat in mats]


def flip(x):
    return x.astype(F32).T.astype(BF16)


def leaf_kernel(near, got, whole, coefs):
    size = near.shape[1] // 2
    whole[...] = near[...] + got[...]
    a, b = ridge_solve([whole[:size], whole[size:]])
    coefs[:size, :] = a
    coefs[size:, :] = b


def pair_kernel(scaling, near, coefs, far, far_got, out):
    size = near.shape[1] // 2
    half = size // 2
    row = lambda *xs: jnp.concatenate(xs, axis=1)
    column = lambda *xs: jnp.concatenate(xs, axis=0)
    far = far[...] + far_got[...]
    corner = column(far[:half, :size], far[:half, size:])
    joint = column(row(near[:size, :size], corner), row(corner.T, near[size:, :size]))
    cross = column(near[:size, size:], near[size:, size:])
    both = coefs[...]
    both_t = flip(both)
    gram = scaling * scaling * dot_wide(both_t, wide_dot(joint, both))
    system = row(gram, scaling * dot_wide(both_t, cross))
    (own,) = ridge_solve([system])
    out[:size, :] = system
    out[size : 2 * size, :] = dot(flip(own), both_t)
    out[2 * size : 2 * size + half, :] = row(own[:half], own[half:]).astype(F32)
    out[2 * size + half :, :] = far[half:, :]


def root_kernel(scaling, place, mine, other, pieces, own, send, table):
    size = mine.shape[1] // 2
    row = lambda *xs: jnp.concatenate(xs, axis=1)
    column = lambda *xs: jnp.concatenate(xs, axis=0)
    low = place[0] == 0
    a, b = mine[size : 2 * size, :], other[size : 2 * size, :]
    p, q = jnp.where(low, a, b), jnp.where(low, b, a)
    last = 5 * size // 2
    a, b = mine[last:, :], other[last:, :]
    corner = column(jnp.where(low, a, b), jnp.where(low, b, a))
    square = scaling * scaling
    exact = dict(precision=lax.Precision.HIGHEST, preferred_element_type=F32)
    right = lax.dot_general(corner, q, (((1,), (1,)), ((), ())), **exact)
    across = (square * square) * jnp.dot(p, right, **exact)
    gram, cross = across + across.T, 0.0
    for half in (mine, other):
        coef = half[2 * size : last, :].astype(BF16)
        coef = column(coef[:, :size], coef[:, size:])
        coef_t = flip(coef)
        gram = gram + square * dot_wide(coef_t, wide_dot(half[:size, :size], coef))
        cross = cross + scaling * dot_wide(coef_t, half[:size, size:])
    (last,) = ridge_solve([row(gram, cross)])
    total_t = dot_wide(flip(last), row(p, q))
    result = (square * scaling) * sum(dot(part, pieces[...]) for part in halves(total_t))
    table[:size, :] = result[:, : 2 * size]
    table[size:, :] = result[:, 2 * size :]
    count = own.shape[0]
    for out, at in ((own, place[1]), (send, place[2])):
        at = pl.multiple_of(at * count, count)
        for i in range(2):
            out[:, i * 2 * size : (i + 1) * 2 * size] = table[pl.ds(at + i * size, count), :]


def local_call(kernel, name, out, *args, scalars=(), scratch=(), flops=1 << 24):
    vmem = pl.BlockSpec(memory_space=pltpu.VMEM)
    smem = pl.BlockSpec(memory_space=pltpu.SMEM)
    return pl.pallas_call(
        kernel,
        in_specs=[smem] * len(scalars) + [vmem] * len(args),
        out_specs=jax.tree.map(lambda _: vmem, out),
        out_shape=out,
        scratch_shapes=scratch,
        compiler_params=pltpu.CompilerParams(vmem_limit_bytes=VMEM_BYTES),
        cost_estimate=pl.CostEstimate(flops=flops, bytes_accessed=1 << 17, transcendentals=0),
        name=name,
    )(*scalars, *args)


def swap(x, axis, mask):
    return lax.ppermute(x, axis, [(i, i ^ mask) for i in range(lax.axis_size(axis))])


def body(probes, sources, sketch, pairing):
    groups, ranks = probes.shape[:2]
    coarse_x = probes.shape[3] // 4
    layer = sketch.shape[2]
    shots, space = lax.axis_size("shots"), lax.axis_size("space")
    shot, place = lax.axis_index("shots"), lax.axis_index("space")
    scaling = math.sqrt(coarse_x * space * layer / ranks)
    side = place % 2

    own, to_core, to_chip = restrict(probes, sources, side[None].astype(jnp.int32))
    from_core = swap(to_core, "space", 1)
    across = [(i, (i + 1 if i % 2 else i - 1) % space) for i in range(space)]
    from_chip = lax.ppermute(to_chip, "space", across)
    from_chip = jnp.where((place == 0) | (place == space - 1), 0.0, from_chip)
    from_below = jnp.where(side == 0, from_chip, from_core)
    from_above = jnp.where(side == 0, from_core, from_chip)
    leaf = (own + jnp.concatenate([from_below, from_above], axis=1)).astype(BF16)

    leaves = [leaf] + [swap(leaf, "shots", m) for m in range(1, shots)]
    picked = shots * groups // 2
    chosen = lax.dynamic_slice_in_dim(pairing, shot // (shots // 2) * picked, picked)
    slots = (chosen // groups ^ shot) * groups + chosen % groups
    sketch_t = jnp.transpose(sketch, (1, 0, 2)).reshape(ranks, coarse_x * layer)
    slots = jnp.concatenate([slots, side[None]]).astype(jnp.int32)
    pieces, near, send, far, send_far = products(leaves, sketch_t, slots, ranks)

    near = near + swap(send, "space", 1)
    far = far + swap(send_far, "space", 1)
    mask = 2
    while 2 * mask < space:
        near, far = near + swap(near, "space", mask), far + swap(far, "space", mask)
        mask *= 2
    near_got, far_got = swap(near, "space", mask), swap(far, "space", mask)
    near, coefs = local_call(
        leaf_kernel, "leaf",
        [
            jax.ShapeDtypeStruct(near.shape, F32),
            jax.ShapeDtypeStruct((2 * ranks, ranks), BF16),
        ],
        near, near_got, flops=1 << 24,
    )
    mine = local_call(
        lambda *refs: pair_kernel(scaling, *refs), "pair",
        jax.ShapeDtypeStruct((7 * ranks // 2, 2 * ranks), F32), near, coefs, far, far_got,
    )
    other = swap(mine, "space", 1)

    columns = ranks // shots
    across_tree = shots // 2
    spots = jnp.stack([side, shot, shot ^ across_tree]).astype(jnp.int32)
    part = jax.ShapeDtypeStruct((columns, pieces.shape[1]), F32)
    own_part, sent = local_call(
        lambda *refs: root_kernel(scaling, *refs), "root", [part, part], mine, other, pieces,
        scalars=(spots,), scratch=[pltpu.VMEM((2 * ranks, 2 * ranks), F32)],
    )
    total = (own_part + swap(sent, "shots", across_tree)).astype(BF16)
    return jnp.transpose(total.reshape(columns, coarse_x, layer), (1, 0, 2))


def solution(mesh):
    in_specs = (
        P("shots", None, None, "space", None, None),
        P("shots", None, "space", None, None),
        P("space", None, None),
        P(),
    )
    out_specs = P("space", "shots", None)
    return jax.shard_map(body, mesh=mesh, in_specs=in_specs, out_specs=out_specs, check_vma=False)
```

```python
import math

import jax
import jax.numpy as jnp
import numpy as np
from jax import lax
from jax.experimental import pallas as pl
from jax.experimental.pallas import tpu as pltpu
from jax.sharding import PartitionSpec as P

F32 = jnp.float32
BF16 = jnp.bfloat16
VMEM_BYTES = 48 << 20
FRONT_VMEM = 24 << 20


def spline_weights(fine_count, coarse_count, coarse_start):
    fine = np.arange(fine_count, dtype=np.float64)
    coarse = np.arange(coarse_count, dtype=np.float64) + coarse_start
    s = np.abs((fine[:, None] + 0.5 - 4.0 * coarse[None, :] - 2.0) / 4.0)
    inner = 2.0 / 3.0 - s**2 + 0.5 * s**3
    outer = np.maximum(2.0 - s, 0.0) ** 3 / 6.0
    return np.where(s < 1.0, inner, outer) / 4.0


def two_terms(table):
    table = jnp.asarray(table, F32)
    high = table.astype(BF16)
    return high, (table - high.astype(F32)).astype(BF16)


def halves(x):
    high = x.astype(BF16)
    return high, (x - high.astype(F32)).astype(BF16)


def thirds(x):
    high = x.astype(BF16)
    rest = x - high.astype(F32)
    mid = rest.astype(BF16)
    return high, mid, (rest - mid.astype(F32)).astype(BF16)


def dot(a, b):
    return jnp.dot(a, b, preferred_element_type=F32)


def dot_nt(a, b):
    return lax.dot_general(a, b, (((1,), (1,)), ((), ())), preferred_element_type=F32)


def wide_dot(wide, exact):
    return sum(dot(part, exact) for part in thirds(wide))


def dot_wide(exact, wide):
    return sum(dot(exact, part) for part in thirds(wide))


def restrict_kernel(
    side, probes, sources, table_xy, table_z, own, to_core, to_chip,
    rows, held, raw, fields, weights_xy, weights_z, arrived, ready,
):
    edges, fine_z = weights_xy.shape[0] // 2, rows.shape[1]
    cells = weights_xy.shape[1] // 2
    all_rows = own.shape[0]
    chunks = arrived.shape[0]
    share = held.shape[0] // chunks
    ranks = share // (2 * cells)
    groups = sources.shape[0]

    def arrival(i):
        part = pl.ds(i * share, share)
        return pltpu.make_async_copy(probes.at[part], held.at[part], arrived.at[i])

    small = [
        pltpu.make_async_copy(source, target, ready.at[i])
        for i, (source, target) in enumerate(
            ((sources, raw), (table_xy, weights_xy), (table_z, weights_z))
        )
    ]
    small[0].start()
    small[1].start()
    ahead = chunks - 1
    for i in range(ahead):
        arrival(i).start()
    small[2].start()
    small[0].wait()
    small[1].wait()
    fields[...] = raw[...].astype(F32)
    for i in range(chunks):
        g = i * groups // chunks
        arrival(i).wait()
        if i + ahead < chunks:
            arrival(i + ahead).start()
        for pair in range(ranks // 2):
            first, second = (i * ranks + 2 * pair + k for k in range(2))
            high, low = ([], []), ([], [])
            for c in range(0, cells, 16):
                field0, field1 = fields[g, c : c + 16], fields[g, cells + c : cells + c + 16]
                for k, rank in enumerate((first, second)):
                    at = rank * 2 * cells + c
                    image = held[at : at + 16].astype(F32) * field0
                    image = image + held[at + cells : at + cells + 16].astype(F32) * field1
                    parts = halves(image)
                    high[k].append(parts[0])
                    low[k].append(parts[1])
            both = jnp.concatenate(
                [jnp.concatenate(high[k] + low[k], axis=0) for k in range(2)], axis=1
            )
            both = dot(weights_xy[...], both)
            both = both[:edges] + both[edges:]
            for k, rank in enumerate((first, second)):
                rows[rank * edges : (rank + 1) * edges, :] = both[:, k * fine_z : (k + 1) * fine_z]
    small[2].wait()
    per = weights_z.shape[0] // fine_z
    lanes = weights_z.shape[1] // 2
    layers = []
    for j in range(edges // per):
        parts = [halves(rows[pl.ds(j * per + r, all_rows, stride=edges), :]) for r in range(per)]
        total = sum(dot(jnp.concatenate(x, axis=1), weights_z[...]) for x in zip(*parts))
        layers.append(total[:, :lanes] + total[:, lanes:])
    own[...] = jnp.concatenate(layers[1:-1], axis=1)
    odd = side[0] == 1
    to_core[...] = jnp.where(odd, layers[0], layers[-1])
    to_chip[...] = jnp.where(odd, layers[-1], layers[0])


def restrict(probes, sources, side):
    groups, ranks, steps_t, fine_x, fine_y, fine_z = probes.shape
    cells = fine_x * fine_y
    coarse_x, coarse_y, coarse_z = fine_x // 4, fine_y // 4, fine_z // 4
    edges_x = coarse_x + 4
    weights_x = spline_weights(fine_x, edges_x, -2)
    weights_y = spline_weights(fine_y, coarse_y, 0)
    weights_z = spline_weights(fine_z, coarse_z, 0)
    table_xy = np.einsum("xe,yd->edxy", weights_x, weights_y).reshape(edges_x * coarse_y, cells)
    high, low = two_terms(table_xy)
    table_xy = jnp.concatenate(
        [jnp.concatenate([high, high], axis=1), jnp.concatenate([low, low], axis=1)], axis=0
    )
    per = 128 // coarse_z
    table_z = np.einsum("zc,rs->rzsc", weights_z, np.eye(per)).reshape(per * fine_z, 128)
    table_z = jnp.concatenate(two_terms(table_z), axis=1)
    all_rows = groups * ranks
    lanes = edges_x * coarse_y * coarse_z - 256
    chunks = 2 * groups
    outside = pl.BlockSpec(memory_space=pltpu.HBM)
    vmem = pl.BlockSpec(memory_space=pltpu.VMEM)
    series = steps_t * cells
    return pl.pallas_call(
        restrict_kernel,
        in_specs=[pl.BlockSpec(memory_space=pltpu.SMEM)] + [outside] * 4,
        out_specs=[vmem] * 3,
        out_shape=[pltpu.VMEM((all_rows, n), F32) for n in (lanes, 128, 128)],
        scratch_shapes=[
            pltpu.VMEM((edges_x * coarse_y * all_rows, fine_z), F32),
            pltpu.VMEM((all_rows * series, fine_z), BF16),
            pltpu.VMEM((groups, series, fine_z), BF16),
            pltpu.VMEM((groups, series, fine_z), F32),
            pltpu.VMEM(table_xy.shape, BF16),
            pltpu.VMEM(table_z.shape, BF16),
            pltpu.SemaphoreType.DMA((chunks,)),
            pltpu.SemaphoreType.DMA((3,)),
        ],
        compiler_params=pltpu.CompilerParams(vmem_limit_bytes=FRONT_VMEM),
        name="restrict",
    )(
        side,
        *(
            pltpu.with_memory_space_constraint(x, pltpu.HBM)
            for x in (
                probes.reshape(all_rows * series, fine_z),
                sources.reshape(groups, series, fine_z),
                table_xy,
                table_z,
            )
        ),
    )


def products_kernel(ranks, place, *refs):
    *leaves, sketch, chosen, keep, send, keep_far, send_far, table = refs
    rows = leaves[0].shape[0]
    for i, leaf in enumerate(leaves):
        table[i * rows : (i + 1) * rows, :] = leaf[...]
    picked = chosen.shape[0] // ranks
    for i in range(picked):
        at = pl.multiple_of(place[i] * ranks, ranks)
        chosen[i * ranks : (i + 1) * ranks, :] = table[pl.ds(at, ranks), :]
    pieces = chosen[...]
    gram = dot_nt(pieces, pieces)
    cross = dot_nt(pieces, sketch[...])
    block = lambda i, j: gram[i * ranks : (i + 1) * ranks, j * ranks : (j + 1) * ranks]
    row = lambda *xs: jnp.concatenate(xs, axis=1)
    solo = lambda i: row(block(i, i), cross[i * ranks : (i + 1) * ranks])
    half = ranks // 2
    fold = lambda x: row(x[:half], x[half:])
    low = place[picked] == 0
    keep[:ranks, :], keep[ranks:, :] = solo(0), solo(1)
    send[:ranks, :], send[ranks:, :] = solo(2), solo(3)
    keep_far[:half, :], send_far[:half, :] = fold(block(0, 1)), fold(block(2, 3))
    across = lambda i, j: row(block(i, j), block(i, j + 1))
    keep_far[half:, :] = jnp.where(low, across(0, 2), across(3, 0))
    send_far[half:, :] = jnp.where(low, across(1, 2), across(2, 0))


def products(leaves, sketch, place, ranks):
    rows, lanes = leaves[0].shape
    count = len(leaves)
    half = (count * rows // ranks // 2) * ranks
    vmem = pl.BlockSpec(memory_space=pltpu.VMEM)
    near = jax.ShapeDtypeStruct((2 * ranks, 2 * ranks), F32)
    far = jax.ShapeDtypeStruct((3 * ranks // 2, 2 * ranks), F32)
    return pl.pallas_call(
        lambda *refs: products_kernel(ranks, *refs),
        in_specs=[pl.BlockSpec(memory_space=pltpu.SMEM)] + [vmem] * (count + 1),
        out_specs=[vmem] * 5,
        out_shape=[jax.ShapeDtypeStruct((half, lanes), BF16), near, near, far, far],
        scratch_shapes=[pltpu.VMEM((count * rows, lanes), BF16)],
        compiler_params=pltpu.CompilerParams(vmem_limit_bytes=VMEM_BYTES),
        name="products",
    )(place, *leaves, sketch)


def ridge_solve(systems):
    size = systems[0].shape[0]
    blocks = size // 8
    shape = (size, 2 * size)
    eye = lax.broadcasted_iota(jnp.int32, shape, 0) == lax.broadcasted_iota(jnp.int32, shape, 1)
    mats = []
    for system in systems:
        trace = jnp.sum(jnp.where(eye, system, 0.0), axis=0, keepdims=True)
        trace = jnp.sum(trace, axis=1, keepdims=True)
        system = system + jnp.where(eye, 0.01 * trace / size + 1e-06, 0.0)
        mats.append([system[8 * i : 8 * i + 8] for i in range(blocks)])
    sub = lax.broadcasted_iota(jnp.int32, (8, 2 * size), 0)
    for k in range(blocks):
        lane = 8 * k
        for mat in mats:
            head = mat[k]
            columns = [
                jnp.broadcast_to(head[:, lane + j : lane + j + 1], head.shape) for j in range(8)
            ]
            for j in range(0, 8, 2):
                left, right = columns[j], columns[j + 1]
                a, b, c = left[j : j + 1], left[j + 1 : j + 2], right[j + 1 : j + 2]
                inverse = 1.0 / (a * c - b * b)

                def reduced(x):
                    p, q = x[j : j + 1], x[j + 1 : j + 2]
                    p, q = (c * p - b * q) * inverse, (a * q - b * p) * inverse
                    rest = (x - left * p) - right * q
                    return jnp.where(sub == j, p, jnp.where(sub == j + 1, q, rest))

                head = reduced(head)
                for m in range(j + 2, 8):
                    columns[m] = reduced(columns[m])
            for i in range(blocks):
                if i != k:
                    new = mat[i]
                    for j in range(8):
                        new = new - mat[i][:, lane + j : lane + j + 1] * head[j : j + 1]
                    mat[i] = new
            mat[k] = head
    return [jnp.concatenate(mat, axis=0)[:, size:].astype(BF16) for mat in mats]


def flip(x):
    return x.astype(F32).T.astype(BF16)


def leaf_kernel(near, got, whole, coefs):
    size = near.shape[1] // 2
    whole[...] = near[...] + got[...]
    a, b = ridge_solve([whole[:size], whole[size:]])
    coefs[:size, :] = a
    coefs[size:, :] = b


def pair_kernel(scaling, near, coefs, far, far_got, out):
    size = near.shape[1] // 2
    half = size // 2
    row = lambda *xs: jnp.concatenate(xs, axis=1)
    column = lambda *xs: jnp.concatenate(xs, axis=0)
    far = far[...] + far_got[...]
    corner = column(far[:half, :size], far[:half, size:])
    joint = column(row(near[:size, :size], corner), row(corner.T, near[size:, :size]))
    cross = column(near[:size, size:], near[size:, size:])
    both = coefs[...]
    both_t = flip(both)
    gram = scaling * scaling * dot_wide(both_t, wide_dot(joint, both))
    system = row(gram, scaling * dot_wide(both_t, cross))
    (own,) = ridge_solve([system])
    out[:size, :] = system
    out[size : 2 * size, :] = dot(flip(own), both_t)
    out[2 * size : 2 * size + half, :] = row(own[:half], own[half:]).astype(F32)
    out[2 * size + half :, :] = far[half:, :]


def root_kernel(scaling, place, mine, other, pieces, own, send, table):
    size = mine.shape[1] // 2
    row = lambda *xs: jnp.concatenate(xs, axis=1)
    column = lambda *xs: jnp.concatenate(xs, axis=0)
    low = place[0] == 0
    a_t, b_t = mine[size : 2 * size, :], other[size : 2 * size, :]
    p, q = jnp.where(low, a_t, b_t), jnp.where(low, b_t, a_t)
    last = 5 * size // 2
    a, b = mine[last:, :], other[last:, :]
    corner = column(jnp.where(low, a, b), jnp.where(low, b, a))
    square = scaling * scaling
    exact = dict(precision=lax.Precision.HIGHEST, preferred_element_type=F32)
    right = lax.dot_general(corner, q, (((1,), (1,)), ((), ())), **exact)
    across = (square * square) * jnp.dot(p, right, **exact)
    gram, cross = across + across.T, 0.0
    for half in (mine, other):
        coef = half[2 * size : last, :].astype(BF16)
        coef = column(coef[:, :size], coef[:, size:])
        coef_t = flip(coef)
        gram = gram + square * dot_wide(coef_t, wide_dot(half[:size, :size], coef))
        cross = cross + scaling * dot_wide(coef_t, half[:size, size:])
    (last,) = ridge_solve([row(gram, cross)])
    table[:size, :size] = last.astype(F32).T
    count = own.shape[0]
    picks = [table[pl.ds(pl.multiple_of(place[i] * count, count), count), :size] for i in (1, 2)]
    total_t = dot_wide(column(*picks).astype(BF16), row(a_t, b_t))
    result = (square * scaling) * sum(dot(part, pieces[...]) for part in halves(total_t))
    own[...] = result[:count]
    send[...] = result[count:]


def local_call(kernel, name, out, *args, scalars=(), scratch=(), flops=1 << 24):
    vmem = pl.BlockSpec(memory_space=pltpu.VMEM)
    smem = pl.BlockSpec(memory_space=pltpu.SMEM)
    return pl.pallas_call(
        kernel,
        in_specs=[smem] * len(scalars) + [vmem] * len(args),
        out_specs=jax.tree.map(lambda _: vmem, out),
        out_shape=out,
        scratch_shapes=scratch,
        compiler_params=pltpu.CompilerParams(vmem_limit_bytes=VMEM_BYTES),
        cost_estimate=pl.CostEstimate(flops=flops, bytes_accessed=1 << 17, transcendentals=0),
        name=name,
    )(*scalars, *args)


def swap(x, axis, mask):
    return lax.ppermute(x, axis, [(i, i ^ mask) for i in range(lax.axis_size(axis))])


def body(probes, sources, sketch, pairing):
    groups, ranks = probes.shape[:2]
    coarse_x = probes.shape[3] // 4
    layer = sketch.shape[2]
    shots, space = lax.axis_size("shots"), lax.axis_size("space")
    shot, place = lax.axis_index("shots"), lax.axis_index("space")
    scaling = math.sqrt(coarse_x * space * layer / ranks)
    side = place % 2

    own, to_core, to_chip = restrict(probes, sources, side[None].astype(jnp.int32))
    from_core = swap(to_core, "space", 1)
    across = [(i, (i + 1 if i % 2 else i - 1) % space) for i in range(space)]
    from_chip = lax.ppermute(to_chip, "space", across)
    from_chip = jnp.where((place == 0) | (place == space - 1), 0.0, from_chip)
    from_below = jnp.where(side == 0, from_chip, from_core)
    from_above = jnp.where(side == 0, from_core, from_chip)
    leaf = (own + jnp.concatenate([from_below, from_above], axis=1)).astype(BF16)

    leaves = [leaf] + [swap(leaf, "shots", m) for m in range(1, shots)]
    picked = shots * groups // 2
    chosen = lax.dynamic_slice_in_dim(pairing, shot // (shots // 2) * picked, picked)
    chosen = lax.dynamic_slice_in_dim(jnp.concatenate([chosen, chosen]), side * (picked // 2), picked)
    slots = (chosen // groups ^ shot) * groups + chosen % groups
    sketch_t = jnp.transpose(sketch, (1, 0, 2)).reshape(ranks, coarse_x * layer)
    slots = jnp.concatenate([slots, side[None]]).astype(jnp.int32)
    pieces, near, send, far, send_far = products(leaves, sketch_t, slots, ranks)

    near = near + swap(send, "space", 1)
    far = far + swap(send_far, "space", 1)
    mask = 2
    while 2 * mask < space:
        near, far = near + swap(near, "space", mask), far + swap(far, "space", mask)
        mask *= 2
    near_got, far_got = swap(near, "space", mask), swap(far, "space", mask)
    near, coefs = local_call(
        leaf_kernel, "leaf",
        [
            jax.ShapeDtypeStruct(near.shape, F32),
            jax.ShapeDtypeStruct((2 * ranks, ranks), BF16),
        ],
        near, near_got, flops=1 << 24,
    )
    mine = local_call(
        lambda *refs: pair_kernel(scaling, *refs), "pair",
        jax.ShapeDtypeStruct((7 * ranks // 2, 2 * ranks), F32), near, coefs, far, far_got,
    )
    other = swap(mine, "space", 1)

    columns = ranks // shots
    across_tree = shots // 2
    spots = jnp.stack([side, shot, shot ^ across_tree]).astype(jnp.int32)
    part = jax.ShapeDtypeStruct((columns, pieces.shape[1]), F32)
    own_part, sent = local_call(
        lambda *refs: root_kernel(scaling, *refs), "root", [part, part], mine, other, pieces,
        scalars=(spots,), scratch=[pltpu.VMEM((ranks, 2 * ranks), F32)],
    )
    total = (own_part + swap(sent, "shots", across_tree)).astype(BF16)
    return jnp.transpose(total.reshape(columns, coarse_x, layer), (1, 0, 2))


def solution(mesh):
    in_specs = (
        P("shots", None, None, "space", None, None),
        P("shots", None, "space", None, None),
        P("space", None, None),
        P(),
    )
    out_specs = P("space", "shots", None)
    return jax.shard_map(body, mesh=mesh, in_specs=in_specs, out_specs=out_specs, check_vma=False)
```

```python
import math

import jax
import jax.numpy as jnp
import numpy as np
from jax import lax
from jax.experimental import pallas as pl
from jax.experimental.pallas import tpu as pltpu
from jax.sharding import PartitionSpec as P

F32 = jnp.float32
BF16 = jnp.bfloat16
VMEM_BYTES = 48 << 20
FRONT_VMEM = 24 << 20


def spline_weights(fine_count, coarse_count, coarse_start):
    fine = np.arange(fine_count, dtype=np.float64)
    coarse = np.arange(coarse_count, dtype=np.float64) + coarse_start
    s = np.abs((fine[:, None] + 0.5 - 4.0 * coarse[None, :] - 2.0) / 4.0)
    inner = 2.0 / 3.0 - s**2 + 0.5 * s**3
    outer = np.maximum(2.0 - s, 0.0) ** 3 / 6.0
    return np.where(s < 1.0, inner, outer) / 4.0


def two_terms(table):
    table = jnp.asarray(table, F32)
    high = table.astype(BF16)
    return high, (table - high.astype(F32)).astype(BF16)


def halves(x):
    high = x.astype(BF16)
    return high, (x - high.astype(F32)).astype(BF16)


def thirds(x):
    high = x.astype(BF16)
    rest = x - high.astype(F32)
    mid = rest.astype(BF16)
    return high, mid, (rest - mid.astype(F32)).astype(BF16)


def dot(a, b):
    return jnp.dot(a, b, preferred_element_type=F32)


def dot_nt(a, b):
    return lax.dot_general(a, b, (((1,), (1,)), ((), ())), preferred_element_type=F32)


def wide_dot(wide, exact):
    return sum(dot(part, exact) for part in thirds(wide))


def dot_wide(exact, wide):
    return sum(dot(exact, part) for part in thirds(wide))


def restrict_kernel(
    side, probes, sources, table_xy, table_z, own, to_core, to_chip,
    rows, held, raw, fields, weights_xy, weights_z, arrived, ready,
):
    edges, fine_z = weights_xy.shape[0] // 2, rows.shape[1]
    cells = weights_xy.shape[1] // 2
    all_rows = own.shape[0]
    chunks = arrived.shape[0]
    share = held.shape[0] // chunks
    ranks = share // (2 * cells)
    groups = sources.shape[0]

    def arrival(i):
        part = pl.ds(i * share, share)
        return pltpu.make_async_copy(probes.at[part], held.at[part], arrived.at[i])

    small = [
        pltpu.make_async_copy(source, target, ready.at[i])
        for i, (source, target) in enumerate(
            ((sources, raw), (table_xy, weights_xy), (table_z, weights_z))
        )
    ]
    small[0].start()
    small[1].start()
    ahead = chunks - 1
    for i in range(ahead):
        arrival(i).start()
    small[2].start()
    small[0].wait()
    small[1].wait()
    fields[...] = raw[...].astype(F32)
    for i in range(chunks):
        g = i * groups // chunks
        arrival(i).wait()
        if i + ahead < chunks:
            arrival(i + ahead).start()
        for pair in range(ranks // 2):
            first, second = (i * ranks + 2 * pair + k for k in range(2))
            high, low = ([], []), ([], [])
            for c in range(0, cells, 16):
                field0, field1 = fields[g, c : c + 16], fields[g, cells + c : cells + c + 16]
                for k, rank in enumerate((first, second)):
                    at = rank * 2 * cells + c
                    image = held[at : at + 16].astype(F32) * field0
                    image = image + held[at + cells : at + cells + 16].astype(F32) * field1
                    parts = halves(image)
                    high[k].append(parts[0])
                    low[k].append(parts[1])
            both = jnp.concatenate(
                [jnp.concatenate(high[k] + low[k], axis=0) for k in range(2)], axis=1
            )
            both = dot(weights_xy[...], both)
            both = both[:edges] + both[edges:]
            for k, rank in enumerate((first, second)):
                rows[rank * edges : (rank + 1) * edges, :] = both[:, k * fine_z : (k + 1) * fine_z]
    small[2].wait()
    per = weights_z.shape[0] // fine_z
    lanes = weights_z.shape[1] // 2
    layers = []
    for j in range(edges // per):
        parts = [halves(rows[pl.ds(j * per + r, all_rows, stride=edges), :]) for r in range(per)]
        total = sum(dot(jnp.concatenate(x, axis=1), weights_z[...]) for x in zip(*parts))
        layers.append(total[:, :lanes] + total[:, lanes:])
    own[...] = jnp.concatenate(layers[1:-1], axis=1)
    odd = side[0] == 1
    to_core[...] = jnp.where(odd, layers[0], layers[-1]).astype(BF16)
    to_chip[...] = jnp.where(odd, layers[-1], layers[0]).astype(BF16)


def restrict(probes, sources, side):
    groups, ranks, steps_t, fine_x, fine_y, fine_z = probes.shape
    cells = fine_x * fine_y
    coarse_x, coarse_y, coarse_z = fine_x // 4, fine_y // 4, fine_z // 4
    edges_x = coarse_x + 4
    weights_x = spline_weights(fine_x, edges_x, -2)
    weights_y = spline_weights(fine_y, coarse_y, 0)
    weights_z = spline_weights(fine_z, coarse_z, 0)
    table_xy = np.einsum("xe,yd->edxy", weights_x, weights_y).reshape(edges_x * coarse_y, cells)
    high, low = two_terms(table_xy)
    table_xy = jnp.concatenate(
        [jnp.concatenate([high, high], axis=1), jnp.concatenate([low, low], axis=1)], axis=0
    )
    per = 128 // coarse_z
    table_z = np.einsum("zc,rs->rzsc", weights_z, np.eye(per)).reshape(per * fine_z, 128)
    table_z = jnp.concatenate(two_terms(table_z), axis=1)
    all_rows = groups * ranks
    lanes = edges_x * coarse_y * coarse_z - 256
    chunks = 2 * groups
    outside = pl.BlockSpec(memory_space=pltpu.HBM)
    vmem = pl.BlockSpec(memory_space=pltpu.VMEM)
    series = steps_t * cells
    return pl.pallas_call(
        restrict_kernel,
        in_specs=[pl.BlockSpec(memory_space=pltpu.SMEM)] + [outside] * 4,
        out_specs=[vmem] * 3,
        out_shape=[
            pltpu.VMEM((all_rows, lanes), F32),
            pltpu.VMEM((all_rows, 128), BF16),
            pltpu.VMEM((all_rows, 128), BF16),
        ],
        scratch_shapes=[
            pltpu.VMEM((edges_x * coarse_y * all_rows, fine_z), F32),
            pltpu.VMEM((all_rows * series, fine_z), BF16),
            pltpu.VMEM((groups, series, fine_z), BF16),
            pltpu.VMEM((groups, series, fine_z), F32),
            pltpu.VMEM(table_xy.shape, BF16),
            pltpu.VMEM(table_z.shape, BF16),
            pltpu.SemaphoreType.DMA((chunks,)),
            pltpu.SemaphoreType.DMA((3,)),
        ],
        compiler_params=pltpu.CompilerParams(vmem_limit_bytes=FRONT_VMEM),
        name="restrict",
    )(
        side,
        *(
            pltpu.with_memory_space_constraint(x, pltpu.HBM)
            for x in (
                probes.reshape(all_rows * series, fine_z),
                sources.reshape(groups, series, fine_z),
                table_xy,
                table_z,
            )
        ),
    )


def products_kernel(ranks, place, *refs):
    *leaves, sketch, chosen, keep, send, keep_far, send_far, table = refs
    rows = leaves[0].shape[0]
    for i, leaf in enumerate(leaves):
        table[i * rows : (i + 1) * rows, :] = leaf[...]
    picked = chosen.shape[0] // ranks
    for i in range(picked):
        at = pl.multiple_of(place[i] * ranks, ranks)
        chosen[i * ranks : (i + 1) * ranks, :] = table[pl.ds(at, ranks), :]
    pieces = chosen[...]
    gram = dot_nt(pieces, pieces)
    cross = dot_nt(pieces, sketch[...])
    block = lambda i, j: gram[i * ranks : (i + 1) * ranks, j * ranks : (j + 1) * ranks]
    row = lambda *xs: jnp.concatenate(xs, axis=1)
    solo = lambda i: row(block(i, i), cross[i * ranks : (i + 1) * ranks])
    half = ranks // 2
    fold = lambda x: row(x[:half], x[half:])
    low = place[picked] == 0
    keep[:ranks, :], keep[ranks:, :] = solo(0), solo(1)
    send[:ranks, :], send[ranks:, :] = solo(2), solo(3)
    keep_far[:half, :], send_far[:half, :] = fold(block(0, 1)), fold(block(2, 3))
    across = lambda i, j: row(block(i, j), block(i, j + 1))
    keep_far[half:, :] = jnp.where(low, across(0, 2), across(3, 0))
    send_far[half:, :] = jnp.where(low, across(1, 2), across(2, 0))


def products(leaves, sketch, place, ranks):
    rows, lanes = leaves[0].shape
    count = len(leaves)
    half = (count * rows // ranks // 2) * ranks
    vmem = pl.BlockSpec(memory_space=pltpu.VMEM)
    near = jax.ShapeDtypeStruct((2 * ranks, 2 * ranks), F32)
    far = jax.ShapeDtypeStruct((3 * ranks // 2, 2 * ranks), F32)
    return pl.pallas_call(
        lambda *refs: products_kernel(ranks, *refs),
        in_specs=[pl.BlockSpec(memory_space=pltpu.SMEM)] + [vmem] * (count + 1),
        out_specs=[vmem] * 5,
        out_shape=[jax.ShapeDtypeStruct((half, lanes), BF16), near, near, far, far],
        scratch_shapes=[pltpu.VMEM((count * rows, lanes), BF16)],
        compiler_params=pltpu.CompilerParams(vmem_limit_bytes=VMEM_BYTES),
        name="products",
    )(place, *leaves, sketch)


def ridge_solve(systems):
    size = systems[0].shape[0]
    blocks = size // 8
    shape = (size, 2 * size)
    eye = lax.broadcasted_iota(jnp.int32, shape, 0) == lax.broadcasted_iota(jnp.int32, shape, 1)
    mats = []
    for system in systems:
        trace = jnp.sum(jnp.where(eye, system, 0.0), axis=0, keepdims=True)
        trace = jnp.sum(trace, axis=1, keepdims=True)
        system = system + jnp.where(eye, 0.01 * trace / size + 1e-06, 0.0)
        mats.append([system[8 * i : 8 * i + 8] for i in range(blocks)])
    sub = lax.broadcasted_iota(jnp.int32, (8, 2 * size), 0)
    for k in range(blocks):
        lane = 8 * k
        for mat in mats:
            head = mat[k]
            columns = [
                jnp.broadcast_to(head[:, lane + j : lane + j + 1], head.shape) for j in range(8)
            ]
            for j in range(0, 8, 2):
                left, right = columns[j], columns[j + 1]
                a, b, c = left[j : j + 1], left[j + 1 : j + 2], right[j + 1 : j + 2]
                inverse = 1.0 / (a * c - b * b)

                def reduced(x):
                    p, q = x[j : j + 1], x[j + 1 : j + 2]
                    p, q = (c * p - b * q) * inverse, (a * q - b * p) * inverse
                    rest = (x - left * p) - right * q
                    return jnp.where(sub == j, p, jnp.where(sub == j + 1, q, rest))

                head = reduced(head)
                for m in range(j + 2, 8):
                    columns[m] = reduced(columns[m])
            for i in range(blocks):
                if i != k:
                    new = mat[i]
                    for j in range(8):
                        new = new - mat[i][:, lane + j : lane + j + 1] * head[j : j + 1]
                    mat[i] = new
            mat[k] = head
    return [jnp.concatenate(mat, axis=0)[:, size:].astype(BF16) for mat in mats]


def flip(x):
    return x.astype(F32).T.astype(BF16)


def leaf_kernel(near, got, whole, coefs):
    size = near.shape[1] // 2
    whole[...] = near[...] + got[...]
    a, b = ridge_solve([whole[:size], whole[size:]])
    coefs[:size, :] = a
    coefs[size:, :] = b


def pair_kernel(scaling, near, coefs, far, far_got, out):
    size = near.shape[1] // 2
    half = size // 2
    row = lambda *xs: jnp.concatenate(xs, axis=1)
    column = lambda *xs: jnp.concatenate(xs, axis=0)
    far = far[...] + far_got[...]
    corner = column(far[:half, :size], far[:half, size:])
    joint = column(row(near[:size, :size], corner), row(corner.T, near[size:, :size]))
    cross = column(near[:size, size:], near[size:, size:])
    both = coefs[...]
    both_t = flip(both)
    gram = scaling * scaling * dot_wide(both_t, wide_dot(joint, both))
    system = row(gram, scaling * dot_wide(both_t, cross))
    (own,) = ridge_solve([system])
    out[:size, :] = system
    out[size : 2 * size, :] = dot(flip(own), both_t)
    out[2 * size : 2 * size + half, :] = row(own[:half], own[half:]).astype(F32)
    out[2 * size + half :, :] = far[half:, :]


def root_kernel(scaling, place, mine, other, pieces, own, send, table):
    size = mine.shape[1] // 2
    row = lambda *xs: jnp.concatenate(xs, axis=1)
    column = lambda *xs: jnp.concatenate(xs, axis=0)
    low = place[0] == 0
    a_t, b_t = mine[size : 2 * size, :], other[size : 2 * size, :]
    p, q = jnp.where(low, a_t, b_t), jnp.where(low, b_t, a_t)
    last = 5 * size // 2
    a, b = mine[last:, :], other[last:, :]
    corner = column(jnp.where(low, a, b), jnp.where(low, b, a))
    square = scaling * scaling
    exact = dict(precision=lax.Precision.HIGHEST, preferred_element_type=F32)
    right = lax.dot_general(corner, q, (((1,), (1,)), ((), ())), **exact)
    across = (square * square) * jnp.dot(p, right, **exact)
    gram, cross = across + across.T, 0.0
    for half in (mine, other):
        coef = half[2 * size : last, :].astype(BF16)
        coef = column(coef[:, :size], coef[:, size:])
        coef_t = flip(coef)
        gram = gram + square * dot_wide(coef_t, wide_dot(half[:size, :size], coef))
        cross = cross + scaling * dot_wide(coef_t, half[:size, size:])
    (last,) = ridge_solve([row(gram, cross)])
    table[:size, :size] = last.astype(F32).T
    count = own.shape[0]
    picks = [table[pl.ds(pl.multiple_of(place[i] * count, count), count), :size] for i in (1, 2)]
    total_t = dot_wide(column(*picks).astype(BF16), row(a_t, b_t))
    result = (square * scaling) * sum(dot(part, pieces[...]) for part in halves(total_t))
    own[...] = result[:count]
    send[...] = result[count:]


def local_call(kernel, name, out, *args, scalars=(), scratch=(), flops=1 << 24):
    vmem = pl.BlockSpec(memory_space=pltpu.VMEM)
    smem = pl.BlockSpec(memory_space=pltpu.SMEM)
    return pl.pallas_call(
        kernel,
        in_specs=[smem] * len(scalars) + [vmem] * len(args),
        out_specs=jax.tree.map(lambda _: vmem, out),
        out_shape=out,
        scratch_shapes=scratch,
        compiler_params=pltpu.CompilerParams(vmem_limit_bytes=VMEM_BYTES),
        cost_estimate=pl.CostEstimate(flops=flops, bytes_accessed=1 << 17, transcendentals=0),
        name=name,
    )(*scalars, *args)


def swap(x, axis, mask):
    return lax.ppermute(x, axis, [(i, i ^ mask) for i in range(lax.axis_size(axis))])


def body(probes, sources, sketch, pairing):
    groups, ranks = probes.shape[:2]
    coarse_x = probes.shape[3] // 4
    layer = sketch.shape[2]
    shots, space = lax.axis_size("shots"), lax.axis_size("space")
    shot, place = lax.axis_index("shots"), lax.axis_index("space")
    scaling = math.sqrt(coarse_x * space * layer / ranks)
    side = place % 2

    own, to_core, to_chip = restrict(probes, sources, side[None].astype(jnp.int32))
    from_core = swap(to_core, "space", 1).astype(F32)
    across = [(i, (i + 1 if i % 2 else i - 1) % space) for i in range(space)]
    from_chip = lax.ppermute(to_chip, "space", across).astype(F32)
    from_chip = jnp.where((place == 0) | (place == space - 1), 0.0, from_chip)
    from_below = jnp.where(side == 0, from_chip, from_core)
    from_above = jnp.where(side == 0, from_core, from_chip)
    leaf = (own + jnp.concatenate([from_below, from_above], axis=1)).astype(BF16)

    leaves = [leaf] + [swap(leaf, "shots", m) for m in range(1, shots)]
    picked = shots * groups // 2
    chosen = lax.dynamic_slice_in_dim(pairing, shot // (shots // 2) * picked, picked)
    chosen = lax.dynamic_slice_in_dim(jnp.concatenate([chosen, chosen]), side * (picked // 2), picked)
    slots = (chosen // groups ^ shot) * groups + chosen % groups
    sketch_t = jnp.transpose(sketch, (1, 0, 2)).reshape(ranks, coarse_x * layer)
    slots = jnp.concatenate([slots, side[None]]).astype(jnp.int32)
    pieces, near, send, far, send_far = products(leaves, sketch_t, slots, ranks)

    near = near + swap(send, "space", 1)
    far = far + swap(send_far, "space", 1)
    mask = 2
    while 2 * mask < space:
        near, far = near + swap(near, "space", mask), far + swap(far, "space", mask)
        mask *= 2
    near_got, far_got = swap(near, "space", mask), swap(far, "space", mask)
    near, coefs = local_call(
        leaf_kernel, "leaf",
        [
            jax.ShapeDtypeStruct(near.shape, F32),
            jax.ShapeDtypeStruct((2 * ranks, ranks), BF16),
        ],
        near, near_got, flops=1 << 24,
    )
    mine = local_call(
        lambda *refs: pair_kernel(scaling, *refs), "pair",
        jax.ShapeDtypeStruct((7 * ranks // 2, 2 * ranks), F32), near, coefs, far, far_got,
    )
    other = swap(mine, "space", 1)

    columns = ranks // shots
    across_tree = shots // 2
    spots = jnp.stack([side, shot, shot ^ across_tree]).astype(jnp.int32)
    part = jax.ShapeDtypeStruct((columns, pieces.shape[1]), F32)
    own_part, sent = local_call(
        lambda *refs: root_kernel(scaling, *refs), "root", [part, part], mine, other, pieces,
        scalars=(spots,), scratch=[pltpu.VMEM((ranks, 2 * ranks), F32)],
    )
    total = (own_part + swap(sent, "shots", across_tree)).astype(BF16)
    return jnp.transpose(total.reshape(columns, coarse_x, layer), (1, 0, 2))


def solution(mesh):
    in_specs = (
        P("shots", None, None, "space", None, None),
        P("shots", None, "space", None, None),
        P("space", None, None),
        P(),
    )
    out_specs = P("space", "shots", None)
    return jax.shard_map(body, mesh=mesh, in_specs=in_specs, out_specs=out_specs, check_vma=False)
```

```python
import math

import jax
import jax.numpy as jnp
import numpy as np
from jax import lax
from jax.experimental import pallas as pl
from jax.experimental.pallas import tpu as pltpu
from jax.sharding import PartitionSpec as P

F32 = jnp.float32
BF16 = jnp.bfloat16
VMEM_BYTES = 48 << 20
FRONT_VMEM = 24 << 20


def spline_weights(fine_count, coarse_count, coarse_start):
    fine = np.arange(fine_count, dtype=np.float64)
    coarse = np.arange(coarse_count, dtype=np.float64) + coarse_start
    s = np.abs((fine[:, None] + 0.5 - 4.0 * coarse[None, :] - 2.0) / 4.0)
    inner = 2.0 / 3.0 - s**2 + 0.5 * s**3
    outer = np.maximum(2.0 - s, 0.0) ** 3 / 6.0
    return np.where(s < 1.0, inner, outer) / 4.0


def two_terms(table):
    table = jnp.asarray(table, F32)
    high = table.astype(BF16)
    return high, (table - high.astype(F32)).astype(BF16)


def halves(x):
    high = x.astype(BF16)
    return high, (x - high.astype(F32)).astype(BF16)


def thirds(x):
    high = x.astype(BF16)
    rest = x - high.astype(F32)
    mid = rest.astype(BF16)
    return high, mid, (rest - mid.astype(F32)).astype(BF16)


def dot(a, b):
    return jnp.dot(a, b, preferred_element_type=F32)


def dot_nt(a, b):
    return lax.dot_general(a, b, (((1,), (1,)), ((), ())), preferred_element_type=F32)


def wide_dot(wide, exact):
    return sum(dot(part, exact) for part in thirds(wide))


def dot_wide(exact, wide):
    return sum(dot(exact, part) for part in thirds(wide))


def restrict_kernel(
    side, probes, sources, table_xy, table_z, own, to_core, to_chip,
    rows, held, raw, fields, weights_xy, weights_z, arrived, ready,
):
    edges, fine_z = weights_xy.shape[0] // 2, rows.shape[1]
    cells = weights_xy.shape[1] // 2
    all_rows = own.shape[0]
    chunks = arrived.shape[0]
    share = held.shape[0] // chunks
    ranks = share // (2 * cells)
    groups = sources.shape[0]

    def arrival(i):
        part = pl.ds(i * share, share)
        return pltpu.make_async_copy(probes.at[part], held.at[part], arrived.at[i])

    small = [
        pltpu.make_async_copy(source, target, ready.at[i])
        for i, (source, target) in enumerate(
            ((sources, raw), (table_xy, weights_xy), (table_z, weights_z))
        )
    ]
    small[0].start()
    small[1].start()
    ahead = chunks - 1
    for i in range(ahead):
        arrival(i).start()
    small[2].start()
    small[0].wait()
    small[1].wait()
    fields[...] = raw[...].astype(F32)
    late = []

    def keep_rows(rank, both):
        both = both[:edges] + both[edges:]
        for k in range(2):
            at = (rank + k) * edges
            rows[at : at + edges, :] = both[:, k * fine_z : (k + 1) * fine_z]

    for i in range(chunks):
        g = i * groups // chunks
        arrival(i).wait()
        if i + ahead < chunks:
            arrival(i + ahead).start()
        for pair in range(ranks // 2):
            first, second = (i * ranks + 2 * pair + k for k in range(2))
            high, low = ([], []), ([], [])
            for c in range(0, cells, 16):
                field0, field1 = fields[g, c : c + 16], fields[g, cells + c : cells + c + 16]
                for k, rank in enumerate((first, second)):
                    at = rank * 2 * cells + c
                    image = held[at : at + 16].astype(F32) * field0
                    image = image + held[at + cells : at + cells + 16].astype(F32) * field1
                    parts = halves(image)
                    high[k].append(parts[0])
                    low[k].append(parts[1])
            both = jnp.concatenate(
                [jnp.concatenate(high[k] + low[k], axis=0) for k in range(2)], axis=1
            )
            late.append((first, dot(weights_xy[...], both)))
            if len(late) > 1:
                keep_rows(*late.pop(0))
    keep_rows(*late.pop(0))
    small[2].wait()
    per = weights_z.shape[0] // fine_z
    lanes = weights_z.shape[1] // 2
    layers = []
    for j in range(edges // per):
        parts = [halves(rows[pl.ds(j * per + r, all_rows, stride=edges), :]) for r in range(per)]
        total = sum(dot(jnp.concatenate(x, axis=1), weights_z[...]) for x in zip(*parts))
        layers.append(total[:, :lanes] + total[:, lanes:])
    own[...] = jnp.concatenate(layers[1:-1], axis=1)
    odd = side[0] == 1
    to_core[...] = jnp.where(odd, layers[0], layers[-1]).astype(BF16)
    to_chip[...] = jnp.where(odd, layers[-1], layers[0]).astype(BF16)


def restrict(probes, sources, side):
    groups, ranks, steps_t, fine_x, fine_y, fine_z = probes.shape
    cells = fine_x * fine_y
    coarse_x, coarse_y, coarse_z = fine_x // 4, fine_y // 4, fine_z // 4
    edges_x = coarse_x + 4
    weights_x = spline_weights(fine_x, edges_x, -2)
    weights_y = spline_weights(fine_y, coarse_y, 0)
    weights_z = spline_weights(fine_z, coarse_z, 0)
    table_xy = np.einsum("xe,yd->edxy", weights_x, weights_y).reshape(edges_x * coarse_y, cells)
    high, low = two_terms(table_xy)
    table_xy = jnp.concatenate(
        [jnp.concatenate([high, high], axis=1), jnp.concatenate([low, low], axis=1)], axis=0
    )
    per = 128 // coarse_z
    table_z = np.einsum("zc,rs->rzsc", weights_z, np.eye(per)).reshape(per * fine_z, 128)
    table_z = jnp.concatenate(two_terms(table_z), axis=1)
    all_rows = groups * ranks
    lanes = edges_x * coarse_y * coarse_z - 256
    chunks = 2 * groups
    outside = pl.BlockSpec(memory_space=pltpu.HBM)
    vmem = pl.BlockSpec(memory_space=pltpu.VMEM)
    series = steps_t * cells
    return pl.pallas_call(
        restrict_kernel,
        in_specs=[pl.BlockSpec(memory_space=pltpu.SMEM)] + [outside] * 4,
        out_specs=[vmem] * 3,
        out_shape=[
            pltpu.VMEM((all_rows, lanes), F32),
            pltpu.VMEM((all_rows, 128), BF16),
            pltpu.VMEM((all_rows, 128), BF16),
        ],
        scratch_shapes=[
            pltpu.VMEM((edges_x * coarse_y * all_rows, fine_z), F32),
            pltpu.VMEM((all_rows * series, fine_z), BF16),
            pltpu.VMEM((groups, series, fine_z), BF16),
            pltpu.VMEM((groups, series, fine_z), F32),
            pltpu.VMEM(table_xy.shape, BF16),
            pltpu.VMEM(table_z.shape, BF16),
            pltpu.SemaphoreType.DMA((chunks,)),
            pltpu.SemaphoreType.DMA((3,)),
        ],
        compiler_params=pltpu.CompilerParams(vmem_limit_bytes=FRONT_VMEM),
        name="restrict",
    )(
        side,
        *(
            pltpu.with_memory_space_constraint(x, pltpu.HBM)
            for x in (
                probes.reshape(all_rows * series, fine_z),
                sources.reshape(groups, series, fine_z),
                table_xy,
                table_z,
            )
        ),
    )


def products_kernel(ranks, place, *refs):
    *leaves, sketch, chosen, keep, send, keep_far, send_far, table = refs
    rows = leaves[0].shape[0]
    for i, leaf in enumerate(leaves):
        table[i * rows : (i + 1) * rows, :] = leaf[...]
    picked = chosen.shape[0] // ranks
    for i in range(picked):
        at = pl.multiple_of(place[i] * ranks, ranks)
        chosen[i * ranks : (i + 1) * ranks, :] = table[pl.ds(at, ranks), :]
    pieces = chosen[...]
    gram = dot_nt(pieces, pieces)
    cross = dot_nt(pieces, sketch[...])
    block = lambda i, j: gram[i * ranks : (i + 1) * ranks, j * ranks : (j + 1) * ranks]
    row = lambda *xs: jnp.concatenate(xs, axis=1)
    solo = lambda i: row(block(i, i), cross[i * ranks : (i + 1) * ranks])
    half = ranks // 2
    fold = lambda x: row(x[:half], x[half:])
    low = place[picked] == 0
    keep[:ranks, :], keep[ranks:, :] = solo(0), solo(1)
    send[:ranks, :], send[ranks:, :] = solo(2), solo(3)
    keep_far[:half, :], send_far[:half, :] = fold(block(0, 1)), fold(block(2, 3))
    across = lambda i, j: row(block(i, j), block(i, j + 1))
    keep_far[half:, :] = jnp.where(low, across(0, 2), across(3, 0))
    send_far[half:, :] = jnp.where(low, across(1, 2), across(2, 0))


def products(leaves, sketch, place, ranks):
    rows, lanes = leaves[0].shape
    count = len(leaves)
    half = (count * rows // ranks // 2) * ranks
    vmem = pl.BlockSpec(memory_space=pltpu.VMEM)
    near = jax.ShapeDtypeStruct((2 * ranks, 2 * ranks), F32)
    far = jax.ShapeDtypeStruct((3 * ranks // 2, 2 * ranks), F32)
    return pl.pallas_call(
        lambda *refs: products_kernel(ranks, *refs),
        in_specs=[pl.BlockSpec(memory_space=pltpu.SMEM)] + [vmem] * (count + 1),
        out_specs=[vmem] * 5,
        out_shape=[jax.ShapeDtypeStruct((half, lanes), BF16), near, near, far, far],
        scratch_shapes=[pltpu.VMEM((count * rows, lanes), BF16)],
        compiler_params=pltpu.CompilerParams(vmem_limit_bytes=VMEM_BYTES),
        name="products",
    )(place, *leaves, sketch)


def ridge_solve(systems):
    size = systems[0].shape[0]
    blocks = size // 8
    shape = (size, 2 * size)
    eye = lax.broadcasted_iota(jnp.int32, shape, 0) == lax.broadcasted_iota(jnp.int32, shape, 1)
    mats = []
    for system in systems:
        trace = jnp.sum(jnp.where(eye, system, 0.0), axis=0, keepdims=True)
        trace = jnp.sum(trace, axis=1, keepdims=True)
        system = system + jnp.where(eye, 0.01 * trace / size + 1e-06, 0.0)
        mats.append([system[8 * i : 8 * i + 8] for i in range(blocks)])
    sub = lax.broadcasted_iota(jnp.int32, (8, 2 * size), 0)
    for k in range(blocks):
        lane = 8 * k
        for mat in mats:
            head = mat[k]
            columns = [
                jnp.broadcast_to(head[:, lane + j : lane + j + 1], head.shape) for j in range(8)
            ]
            for j in range(0, 8, 2):
                left, right = columns[j], columns[j + 1]
                a, b, c = left[j : j + 1], left[j + 1 : j + 2], right[j + 1 : j + 2]
                inverse = 1.0 / (a * c - b * b)

                def reduced(x):
                    p, q = x[j : j + 1], x[j + 1 : j + 2]
                    p, q = (c * p - b * q) * inverse, (a * q - b * p) * inverse
                    rest = (x - left * p) - right * q
                    return jnp.where(sub == j, p, jnp.where(sub == j + 1, q, rest))

                head = reduced(head)
                for m in range(j + 2, 8):
                    columns[m] = reduced(columns[m])
            for i in range(blocks):
                if i != k:
                    new = mat[i]
                    for j in range(8):
                        new = new - mat[i][:, lane + j : lane + j + 1] * head[j : j + 1]
                    mat[i] = new
            mat[k] = head
    return [jnp.concatenate(mat, axis=0)[:, size:].astype(BF16) for mat in mats]


def flip(x):
    return x.astype(F32).T.astype(BF16)


def leaf_kernel(near, got, whole, coefs):
    size = near.shape[1] // 2
    whole[...] = near[...] + got[...]
    a, b = ridge_solve([whole[:size], whole[size:]])
    coefs[:size, :] = a
    coefs[size:, :] = b


def pair_kernel(scaling, near, coefs, far, far_got, out):
    size = near.shape[1] // 2
    half = size // 2
    row = lambda *xs: jnp.concatenate(xs, axis=1)
    column = lambda *xs: jnp.concatenate(xs, axis=0)
    far = far[...] + far_got[...]
    corner = column(far[:half, :size], far[:half, size:])
    joint = column(row(near[:size, :size], corner), row(corner.T, near[size:, :size]))
    cross = column(near[:size, size:], near[size:, size:])
    both = coefs[...]
    both_t = flip(both)
    gram = scaling * scaling * dot_wide(both_t, wide_dot(joint, both))
    system = row(gram, scaling * dot_wide(both_t, cross))
    (own,) = ridge_solve([system])
    out[:size, :] = system
    out[size : 2 * size, :] = dot(flip(own), both_t)
    out[2 * size : 2 * size + half, :] = row(own[:half], own[half:]).astype(F32)
    out[2 * size + half :, :] = far[half:, :]


def root_kernel(scaling, place, mine, other, pieces, own, send, table):
    size = mine.shape[1] // 2
    row = lambda *xs: jnp.concatenate(xs, axis=1)
    column = lambda *xs: jnp.concatenate(xs, axis=0)
    low = place[0] == 0
    a_t, b_t = mine[size : 2 * size, :], other[size : 2 * size, :]
    p, q = jnp.where(low, a_t, b_t), jnp.where(low, b_t, a_t)
    last = 5 * size // 2
    a, b = mine[last:, :], other[last:, :]
    corner = column(jnp.where(low, a, b), jnp.where(low, b, a))
    square = scaling * scaling
    exact = dict(precision=lax.Precision.HIGHEST, preferred_element_type=F32)
    right = lax.dot_general(corner, q, (((1,), (1,)), ((), ())), **exact)
    across = (square * square) * jnp.dot(p, right, **exact)
    gram, cross = across + across.T, 0.0
    for half in (mine, other):
        coef = half[2 * size : last, :].astype(BF16)
        coef = column(coef[:, :size], coef[:, size:])
        coef_t = flip(coef)
        gram = gram + square * dot_wide(coef_t, wide_dot(half[:size, :size], coef))
        cross = cross + scaling * dot_wide(coef_t, half[:size, size:])
    (last,) = ridge_solve([row(gram, cross)])
    table[:size, :size] = last.astype(F32).T
    count = own.shape[0]
    picks = [table[pl.ds(pl.multiple_of(place[i] * count, count), count), :size] for i in (1, 2)]
    total_t = dot_wide(column(*picks).astype(BF16), row(a_t, b_t))
    result = (square * scaling) * sum(dot(part, pieces[...]) for part in halves(total_t))
    own[...] = result[:count]
    send[...] = result[count:]


def local_call(kernel, name, out, *args, scalars=(), scratch=(), flops=1 << 24):
    vmem = pl.BlockSpec(memory_space=pltpu.VMEM)
    smem = pl.BlockSpec(memory_space=pltpu.SMEM)
    return pl.pallas_call(
        kernel,
        in_specs=[smem] * len(scalars) + [vmem] * len(args),
        out_specs=jax.tree.map(lambda _: vmem, out),
        out_shape=out,
        scratch_shapes=scratch,
        compiler_params=pltpu.CompilerParams(vmem_limit_bytes=VMEM_BYTES),
        cost_estimate=pl.CostEstimate(flops=flops, bytes_accessed=1 << 17, transcendentals=0),
        name=name,
    )(*scalars, *args)


def swap(x, axis, mask):
    return lax.ppermute(x, axis, [(i, i ^ mask) for i in range(lax.axis_size(axis))])


def body(probes, sources, sketch, pairing):
    groups, ranks = probes.shape[:2]
    coarse_x = probes.shape[3] // 4
    layer = sketch.shape[2]
    shots, space = lax.axis_size("shots"), lax.axis_size("space")
    shot, place = lax.axis_index("shots"), lax.axis_index("space")
    scaling = math.sqrt(coarse_x * space * layer / ranks)
    side = place % 2

    own, to_core, to_chip = restrict(probes, sources, side[None].astype(jnp.int32))
    from_core = swap(to_core, "space", 1).astype(F32)
    across = [(i, (i + 1 if i % 2 else i - 1) % space) for i in range(space)]
    from_chip = lax.ppermute(to_chip, "space", across).astype(F32)
    from_chip = jnp.where((place == 0) | (place == space - 1), 0.0, from_chip)
    from_below = jnp.where(side == 0, from_chip, from_core)
    from_above = jnp.where(side == 0, from_core, from_chip)
    leaf = (own + jnp.concatenate([from_below, from_above], axis=1)).astype(BF16)

    leaves = [leaf] + [swap(leaf, "shots", m) for m in range(1, shots)]
    picked = shots * groups // 2
    chosen = lax.dynamic_slice_in_dim(pairing, shot // (shots // 2) * picked, picked)
    chosen = lax.dynamic_slice_in_dim(jnp.concatenate([chosen, chosen]), side * (picked // 2), picked)
    slots = (chosen // groups ^ shot) * groups + chosen % groups
    sketch_t = jnp.transpose(sketch, (1, 0, 2)).reshape(ranks, coarse_x * layer)
    slots = jnp.concatenate([slots, side[None]]).astype(jnp.int32)
    pieces, near, send, far, send_far = products(leaves, sketch_t, slots, ranks)

    near = near + swap(send, "space", 1)
    far = far + swap(send_far, "space", 1)
    mask = 2
    while 2 * mask < space:
        near, far = near + swap(near, "space", mask), far + swap(far, "space", mask)
        mask *= 2
    near_got, far_got = swap(near, "space", mask), swap(far, "space", mask)
    near, coefs = local_call(
        leaf_kernel, "leaf",
        [
            jax.ShapeDtypeStruct(near.shape, F32),
            jax.ShapeDtypeStruct((2 * ranks, ranks), BF16),
        ],
        near, near_got, flops=1 << 24,
    )
    mine = local_call(
        lambda *refs: pair_kernel(scaling, *refs), "pair",
        jax.ShapeDtypeStruct((7 * ranks // 2, 2 * ranks), F32), near, coefs, far, far_got,
    )
    other = swap(mine, "space", 1)

    columns = ranks // shots
    across_tree = shots // 2
    spots = jnp.stack([side, shot, shot ^ across_tree]).astype(jnp.int32)
    part = jax.ShapeDtypeStruct((columns, pieces.shape[1]), F32)
    own_part, sent = local_call(
        lambda *refs: root_kernel(scaling, *refs), "root", [part, part], mine, other, pieces,
        scalars=(spots,), scratch=[pltpu.VMEM((ranks, 2 * ranks), F32)],
    )
    total = (own_part + swap(sent, "shots", across_tree)).astype(BF16)
    return jnp.transpose(total.reshape(columns, coarse_x, layer), (1, 0, 2))


def solution(mesh):
    in_specs = (
        P("shots", None, None, "space", None, None),
        P("shots", None, "space", None, None),
        P("space", None, None),
        P(),
    )
    out_specs = P("space", "shots", None)
    return jax.shard_map(body, mesh=mesh, in_specs=in_specs, out_specs=out_specs, check_vma=False)
```
